256 devices in a mesh: dp: 64 (over z, x, core), feat: 4 (over y).
Axes of the slice: x: 4, y: 4, z: 8, core: 2. Of those that a mesh axis runs over, the one named last changes fastest.
Arguments:
- member_feats: bfloat16 [262144, 256], P(('dp', 'feat')), may hold values from -6 to 6
- labels: int32 [262144], P(('dp', 'feat')), may hold values 0 or 1
- fixed_values: bfloat16 [262144, 2048], P('dp', 'feat'), may hold values from -6 to 6
- fixed_blocks: int32 [262144, 4], P('dp', 'feat'), may hold values from 0 to 511
- fixed_coef: float32 [2048, 512], P('feat'), may hold values from -0.12 to 0.12
- member_coef: float32 [1024, 256], P(('dp', 'feat')), may hold values from -0.36 to 0.36
- row_slot: int32 [262144], P(('dp', 'feat')), may hold values from 0 to 2047, as said below
- tile_source: int32 [622592], P(('dp', 'feat')), may hold values from 0 to 2048, as said below
- member_tiles: int32 [1024], P(('dp', 'feat')), may hold values from 1 to 16, as said below
Outputs:
- margin: float32 [262144], P(('dp', 'feat'))
- updated_coef: float32 [1024, 256], P(('dp', 'feat'))
- fixed_grad: float32 [2048, 512], P('feat')
The draws below stay inside these ranges and needn't reach their ends.
Inputs may be any that keep to these rules, and one draw needn't show every extreme that they name: `row_slot`: each owner receives the same number of rows, 32, 16 or 8, from every device of its feat column; some owner receives 32 from every device. The rows one device sends to one owner take that owner's slots 0, 1, 2 and so on, each slot once. `tile_source`: every received row appears at exactly one position. An owner's members, in order, take consecutive runs of tiles; a member's rows fill its tiles from the first position on, and the rest of its last tile is padding, as are the tiles past all members. `member_tiles`: A member's tiles are its received rows divided by 128, rounded up; a device's members use at most 19 tiles in all, exactly 19 on the owners that receive 32 rows from every device.
All inputs are finite; a program needn't handle non-finite values. No bound on the sum of `labels` on one device may be relied on, other than what follows from the above.
Results may differ from the reference program's by a relative error of at most 0.0013.
Values may be sent and summed in bfloat16 or wider, within the bound.
A program may use at most 64 MiB of HBM per device.

```python
import jax
import jax.numpy as jnp
from jax import lax

RE_DIM = 256
BLOCK = 512
FE_BLOCKS = 2048
ROWS_DEV = 1024
MEM_DEV = 4
CG_ITERS = 2
TILE = 128
CAP = 32
TILES_DEV = 19
ROWS = 262144
MEMBERS = 1024
FE_COLS = 2048
N_DP = 64
N_FEAT = 4


def layout(key):
    device_total = N_DP * N_FEAT
    slot_total = N_DP * CAP
    tiled_rows = TILES_DEV * TILE
    level_table = jnp.array([CAP, CAP // 2, CAP // 4, CAP // 4], dtype=jnp.int32)
    column_keys = jax.random.split(jax.random.fold_in(key, 1), N_FEAT)

    def column_classes(column_key):
        shuffled = jax.random.permutation(column_key, N_DP).astype(jnp.int32)
        return ((shuffled - shuffled[N_DP - 1]) % 4).astype(jnp.int32)
    classes = jax.vmap(column_classes)(column_keys)
    counts = level_table[classes]
    sender_keys = jax.random.split(jax.random.fold_in(key, 2), device_total)
    owner_keys = jax.random.split(jax.random.fold_in(key, 3), device_total)

    def sender(sender_key, device):
        per_owner = counts[device % N_FEAT]
        owner_ends = jnp.cumsum(per_owner)
        ordinal = jnp.arange(ROWS_DEV, dtype=jnp.int32)
        owner_index = jnp.sum((ordinal[:, None] >= owner_ends[None, :]).astype(jnp.int32), axis=1)
        slot_index = ordinal - (owner_ends - per_owner)[owner_index]
        slot_value = (owner_index * CAP + slot_index).astype(jnp.int32)
        shuffle = jax.random.permutation(sender_key, ROWS_DEV)
        return jnp.zeros((ROWS_DEV,), jnp.int32).at[shuffle].set(slot_value)

    def owner_side(owner_key, device):
        per_source = counts[device % N_FEAT, device // N_FEAT]
        received = N_DP * per_source
        most_extra = jnp.maximum(0, (received - MEM_DEV) // (TILE * (MEM_DEV - 1)))
        extra_tiles = jax.random.randint(owner_key, (MEM_DEV - 1,), 0, most_extra + 1).astype(jnp.int32)
        keep_extra = (device // N_FEAT != N_DP - 1).astype(jnp.int32)
        extra_tiles = (extra_tiles * keep_extra).astype(jnp.int32)
        leading_rows = TILE * extra_tiles + 1
        member_rows = jnp.concatenate([leading_rows, (received - jnp.sum(leading_rows))[None]]).astype(jnp.int32)
        tiles_of = ((member_rows + TILE - 1) // TILE).astype(jnp.int32)
        row_ends = jnp.cumsum(member_rows)
        row_start = row_ends - member_rows
        tile_start = jnp.cumsum(tiles_of) - tiles_of
        ordinal = jnp.arange(slot_total, dtype=jnp.int32)
        is_valid = ordinal < received
        member_index = jnp.minimum(jnp.sum((ordinal[:, None] >= row_ends[None, :]).astype(jnp.int32), axis=1), MEM_DEV - 1)
        position = tile_start[member_index] * TILE + ordinal - row_start[member_index]
        position = jnp.where(is_valid, position, tiled_rows).astype(jnp.int32)
        source_slot = (ordinal // per_source * CAP + ordinal % per_source).astype(jnp.int32)
        source_table = jnp.full((tiled_rows,), slot_total, jnp.int32).at[position].set(source_slot, mode='drop')
        return (source_table, tiles_of)
    devices = jnp.arange(device_total, dtype=jnp.int32)
    row_slot = jax.vmap(sender)(sender_keys, devices).reshape(-1)
    source_table, tiles_of = jax.vmap(owner_side)(owner_keys, devices)
    return (row_slot, source_table.reshape(-1), tiles_of.reshape(-1))


def draw_row_slot(key, part):
    return layout(jax.random.fold_in(key, 17))[0]


def draw_tile_source(key, part):
    return layout(jax.random.fold_in(key, 17))[1]


def draw_member_tiles(key, part):
    return layout(jax.random.fold_in(key, 17))[2]


def touch_ends(result, stream_key, least, top_value):
    shape = result.shape
    place = [jax.random.randint(jax.random.fold_in(stream_key, axis), (), 0, shape[axis]) for axis in range(len(shape))]
    result = result.at[tuple(place)].set(least)
    longest = shape.index(max(shape))
    place[longest] = (place[longest] + 1) % shape[longest]
    return result.at[tuple(place)].set(top_value)


def block_levels(own_key, shape, pieces, least, high):
    def one(dim, shards_of):
        steps = jax.random.uniform(jax.random.fold_in(jax.random.fold_in(own_key, 6), dim), (shards_of,), jnp.float32, least / len(pieces), high / len(pieces))
        return jnp.repeat(jnp.exp(steps), shape[dim] // shards_of).reshape((-1,) + (1,) * (len(shape) - dim - 1))

    level = one(*pieces[0])
    for cut in pieces[1:]:
        level = level * one(*cut)
    return level


def normal_values(key, dims, spread, most, cuts=(), held_as=jnp.bfloat16):
    result = jax.random.normal(key, dims, jnp.float32) * spread
    if len(cuts) > 0:
        result = block_levels(key, dims, cuts, -0.22, 0.18) * result
    return jnp.clip(result, min=-most, max=most).astype(held_as)


def setup_inputs(seed: int = 0) -> dict:
    streams_of = jax.random.split(jax.random.key(seed), 10)
    return {
        "member_feats": normal_values(streams_of[0], (ROWS, RE_DIM), 1.0, 6.0, ((0, 256),)),
        "labels": touch_ends((jax.random.randint(streams_of[1], (ROWS,), 0, 4) < 1).astype(jnp.int32), jax.random.fold_in(streams_of[1], 1), 0, 1),
        "fixed_values": normal_values(streams_of[2], (ROWS, FE_COLS), 1.0, 6.0, ((0, 64), (1, 4))),
        "fixed_blocks": touch_ends(jax.random.randint(streams_of[3], (ROWS, N_FEAT), 0, FE_BLOCKS // N_FEAT), jax.random.fold_in(streams_of[3], 1), 0, (FE_BLOCKS // N_FEAT) - 1).astype(jnp.int32),
        "fixed_coef": normal_values(streams_of[4], (FE_BLOCKS, BLOCK), 0.02, 0.12, ((0, 4),), jnp.float32),
        "member_coef": normal_values(streams_of[5], (MEMBERS, RE_DIM), 0.06, 0.36, ((0, 256),), jnp.float32),
        "row_slot": draw_row_slot(jax.random.fold_in(streams_of[9], 71), 0),
        "tile_source": draw_tile_source(jax.random.fold_in(streams_of[9], 71), 0),
        "member_tiles": draw_member_tiles(jax.random.fold_in(streams_of[9], 71), 0),
    }


ridge_member = 1.0
ridge_fixed = 1.0
highest = lax.Precision.HIGHEST

def member_update(tiled_feats, tiled_fixed, tiled_label, coef, tile_counts):
    tile_total = tiled_feats.shape[0] // TILE
    feats_wide = tiled_feats.astype(jnp.float32).reshape(tile_total, TILE, RE_DIM)
    tile_fixed = tiled_fixed.astype(jnp.float32).reshape(tile_total, TILE)
    tile_label = tiled_label.astype(jnp.float32).reshape(tile_total, TILE)
    tile_ends = jnp.cumsum(tile_counts)
    positions = jnp.arange(tile_total, dtype=jnp.int32)
    member_index = lax.optimization_barrier(jnp.sum((positions[:, None] >= tile_ends[None, :]).astype(jnp.int32), axis=1))
    tile_member = (member_index[:, None] == jnp.arange(MEM_DEV, dtype=jnp.int32)[None, :]).astype(jnp.float32)
    tile_coef = jnp.dot(tile_member, coef, precision=highest)
    logits = tile_fixed + jnp.einsum('tri,ti->tr', feats_wide, tile_coef, precision=highest)
    probability = jax.nn.sigmoid(logits)
    weight = probability * (1.0 - probability)
    gradient = jnp.dot(tile_member.T, jnp.einsum('tr,tri->ti', tile_label - probability, feats_wide, precision=highest), precision=highest) - ridge_member * coef
    diagonal = jnp.dot(tile_member.T, jnp.einsum('tr,tri->ti', weight, feats_wide * feats_wide, precision=highest), precision=highest) + ridge_member
    weighted = feats_wide * weight[:, :, None]
    tile_grams = jnp.einsum('tri,trj->tij', feats_wide, weighted, precision=highest)
    hessian = jnp.einsum('tm,tij->mij', tile_member, tile_grams, precision=highest)
    step_sum = jnp.zeros_like(coef)
    remain = gradient
    scaled = remain / diagonal
    search = scaled
    inner_product = lax.optimization_barrier(jnp.sum(remain * scaled, axis=1))
    for iteration in range(CG_ITERS):
        image = jnp.einsum('mij,mj->mi', hessian, search, precision=highest) + ridge_member * search
        alpha_step = inner_product / lax.optimization_barrier(jnp.sum(search * image, axis=1))
        step_sum = step_sum + alpha_step[:, None] * search
        if iteration + 1 < CG_ITERS:
            remain = remain - alpha_step[:, None] * image
            scaled = remain / diagonal
            inner_next = lax.optimization_barrier(jnp.sum(remain * scaled, axis=1))
            search = scaled + (inner_next / inner_product)[:, None] * search
            inner_product = inner_next
    updated = coef + step_sum
    new_scores = jnp.einsum('tri,ti->tr', feats_wide, jnp.dot(tile_member, updated, precision=highest), precision=highest)
    return (updated, new_scores.reshape(-1))

def reference(member_feats, labels, fixed_values, fixed_blocks, fixed_coef, member_coef, row_slot, tile_source, member_tiles):
    shard_blocks = FE_BLOCKS // N_FEAT
    group_rows = N_FEAT * ROWS_DEV
    slot_total = N_DP * CAP
    device_total = N_DP * N_FEAT
    coef_shards = fixed_coef.reshape(N_FEAT, shard_blocks, BLOCK)

    def group_score(operands):
        values, indices = operands
        values = values.reshape(group_rows, N_FEAT, BLOCK)
        total = jnp.zeros((group_rows,), jnp.float32)
        for shard in range(N_FEAT):
            looked_up = jnp.take(coef_shards[shard], indices[:, shard], axis=0)
            total = total + lax.optimization_barrier(jnp.sum(values[:, shard, :].astype(jnp.float32) * looked_up, axis=1))
        return total
    fixed_score = lax.map(group_score, (fixed_values.reshape(N_DP, group_rows, N_FEAT * BLOCK), fixed_blocks.reshape(N_DP, group_rows, N_FEAT))).reshape(ROWS)
    row_device = (jnp.arange(ROWS, dtype=jnp.int32) // ROWS_DEV).astype(jnp.int32)
    owner_device = row_slot // CAP * N_FEAT + row_device % N_FEAT
    received_at = row_device // N_FEAT * CAP + row_slot % CAP
    flat_index = (owner_device * (slot_total + 1) + received_at).astype(jnp.int32)
    recv_feats = jnp.zeros((device_total * (slot_total + 1), RE_DIM), jnp.bfloat16).at[flat_index].set(member_feats).reshape(device_total, slot_total + 1, RE_DIM)
    recv_score = jnp.zeros((device_total * (slot_total + 1),), jnp.bfloat16).at[flat_index].set(fixed_score.astype(jnp.bfloat16)).reshape(device_total, slot_total + 1)
    recv_label = jnp.zeros((device_total * (slot_total + 1),), jnp.bfloat16).at[flat_index].set(labels.astype(jnp.bfloat16)).reshape(device_total, slot_total + 1)

    def owner_work(operands):
        feats_here, score_here, label_here, source_here, coef_here, count_here = operands
        updated, new_scores = member_update(feats_here[source_here], score_here[source_here], label_here[source_here], coef_here, count_here)
        back = jnp.zeros((slot_total + 1,), jnp.float32).at[source_here].set(new_scores)
        return (updated, back)
    updated_coef, back = lax.map(owner_work, (recv_feats, recv_score, recv_label, tile_source.reshape(device_total, TILES_DEV * TILE), member_coef.reshape(device_total, MEM_DEV, RE_DIM), member_tiles.reshape(device_total, MEM_DEV)))
    member_score = back.reshape(-1)[flat_index]
    margin = fixed_score + member_score
    residual = labels.astype(jnp.float32) - jax.nn.sigmoid(margin)

    def group_grad(carry, operands):
        values, indices, group_residual = operands
        values = values.reshape(group_rows, N_FEAT, BLOCK)
        parts = jnp.stack([jax.ops.segment_sum(group_residual[:, None] * values[:, shard, :].astype(jnp.float32), indices[:, shard], num_segments=shard_blocks) for shard in range(N_FEAT)])
        return (carry + parts, None)
    total_grad, unused = lax.scan(group_grad, jnp.zeros((N_FEAT, shard_blocks, BLOCK), jnp.float32), (fixed_values.reshape(N_DP, group_rows, N_FEAT * BLOCK), fixed_blocks.reshape(N_DP, group_rows, N_FEAT), residual.reshape(N_DP, group_rows)))
    fixed_grad = ridge_fixed * fixed_coef - total_grad.reshape(FE_BLOCKS, BLOCK) / N_DP
    return (margin, updated_coef.reshape(MEMBERS, RE_DIM), fixed_grad)
```

```python
import functools

import jax
import jax.numpy as jnp
from jax import lax
from jax.experimental import pallas as pl
from jax.experimental.pallas import tpu as pltpu
from jax.sharding import PartitionSpec as P

CG_ITERS = 2
TILE = 128
LANES = 128
RIDGE_MEMBER = 1.0
RIDGE_FIXED = 1.0
F32 = jnp.float32
BF16 = jnp.bfloat16
MESH = pl.DeviceIdType.MESH


def dot_nn(a, b):
    return lax.dot_general(a, b, (((1,), (0,)), ((), ())), preferred_element_type=F32)


def dot_nt(a, b):
    return lax.dot_general(a, b, (((1,), (1,)), ((), ())), preferred_element_type=F32)


def dot_tn(a, b):
    return lax.dot_general(a, b, (((0,), (0,)), ((), ())), preferred_element_type=F32)


def split2(x):
    top = x.astype(BF16)
    return top, (x - top.astype(F32)).astype(BF16)


def iota(shape, dim):
    return lax.broadcasted_iota(jnp.int32, shape, dim)


def as_bf16(mask):
    return jnp.where(mask, 1.0, 0.0).astype(BF16)


def as_f32(mask):
    return jnp.where(mask, 1.0, 0.0).astype(F32)


def grid_of(dp):
    return (8, 4, 2) if dp == 64 else (dp // 4, 2, 2)


def kernel(
    dp,
    feat,
    cap,
    feats,
    labels,
    fv,
    fb,
    fc,
    mcoef,
    rslot,
    tsrc,
    mtiles,
    margin_out,
    coef_out,
    grad_out,
    send_x,
    recv_x,
    send_p,
    recv_p,
    send_s,
    recv_s,
    send_r,
    recv_r,
    send_e,
    recv_e,
    coef_parts,
    member_mask,
    acc,
    recv_c,
    recv_rx,
    recv_rz,
    sx,
    rx,
    sp,
    rp,
    ss,
    rs,
    sr,
    rr,
    se,
    re,
    sc,
    rc,
    srx,
    rrx,
    srz,
    rrz,
    sgz,
    rgz,
    sgx,
    rgx,
    sgc,
    rgc,
):
    planes, chips, cores = grid_of(dp)
    rows = feats.shape[0]
    slots = dp * cap
    cap_bits = cap.bit_length() - 1
    block_count, block_width = fc.shape
    plane_owners = chips * cores
    plane_slots = plane_owners * cap
    i = lax.axis_index("dp")
    f = lax.axis_index("feat")
    z = i // plane_owners
    x = (i % plane_owners) // cores
    c = i % cores

    def at(dp_index, feat_index=None):
        return (dp_index, f if feat_index is None else feat_index)

    barrier = pltpu.get_barrier_semaphore()

    def greet_dp(k, carry):
        pl.semaphore_signal(barrier, inc=1, device_id=at((i + k) % dp), device_id_type=MESH)
        return carry

    lax.fori_loop(1, dp, greet_dp, 0)
    for k in range(1, feat):
        pl.semaphore_signal(
            barrier, inc=1, device_id=at(i, (f + k) % feat), device_id_type=MESH
        )
    pl.semaphore_wait(barrier, dp - 1 + feat - 1)

    slot_row = rslot[...]
    feats_here = feats[...]

    def send_plane(k, carry):
        plane = (z + k) % planes
        base = plane * plane_slots
        pick = as_bf16(slot_row - base == iota((plane_slots, rows), 0))
        picked = dot_nn(pick, feats_here).astype(BF16)
        send_x[pl.ds(plane * plane_owners, plane_owners)] = picked.reshape(
            plane_owners, cap, feats.shape[1]
        )

        def send_owner(q, inner):
            owner = plane * plane_owners + (i + q) % plane_owners

            @pl.when(owner != i)
            def _():
                pltpu.make_async_remote_copy(
                    src_ref=send_x.at[owner],
                    dst_ref=recv_x.at[i],
                    send_sem=sx,
                    recv_sem=rx,
                    device_id=at(owner),
                    device_id_type=MESH,
                ).start()

            return inner

        return lax.fori_loop(0, plane_owners, send_owner, carry)

    lax.fori_loop(0, planes, send_plane, 0)
    recv_x[i] = send_x[i]

    group_rows = feat * rows
    step = min(512, rows)
    coef_parts[0], coef_parts[1] = split2(fc[...])

    def partial_chunk(q, carry):
        start = pl.multiple_of(q * step, step)
        values = fv[pl.ds(start, step), :]
        scores = dot_nt(coef_parts[0], values) + dot_nt(coef_parts[1], values)
        hot = fb[:, pl.ds(start, step)] == iota((block_count, step), 0)
        part = jnp.sum(jnp.where(hot, scores, 0.0), axis=0, keepdims=True)
        per = rows // step
        inner = pl.multiple_of((q % per) * step, step)
        send_p[q // per, :, pl.ds(inner, step)] = part
        return carry

    lax.fori_loop(0, group_rows // step, partial_chunk, 0)
    for k in range(1, feat):
        other = (f + k) % feat
        pltpu.make_async_remote_copy(
            src_ref=send_p.at[other],
            dst_ref=recv_p.at[f],
            send_sem=sp,
            recv_sem=rp,
            device_id=at(i, other),
            device_id_type=MESH,
        ).start()
    recv_p[f] = send_p[f]

    positions = tsrc.shape[1]
    tile = iota((1, positions), 1) >> (TILE.bit_length() - 1)
    members = mcoef.shape[0]
    member = jnp.zeros((1, positions), jnp.int32)
    end = jnp.int32(0)
    for m in range(members):
        end = end + mtiles[m]
        member = member + jnp.where(tile >= end, 1, 0)
    source = tsrc[...]
    code = (member << cap_bits) + (source & (cap - 1))
    code_hot = as_bf16(code == iota((members * cap, positions), 0))
    sender_hot = as_bf16((source >> cap_bits) == iota((dp, positions), 0))
    counted = dot_nt(code_hot, sender_hot).astype(BF16)
    spread = as_bf16((iota((dp, slots), 1) >> cap_bits) == iota((dp, slots), 0))
    slot_mask = as_f32((iota((cap, slots), 1) & (cap - 1)) == iota((cap, slots), 0))
    widened = dot_nn(counted, spread)
    for m in range(members):
        member_mask[pl.ds(m, 1), :] = jnp.sum(
            widened[m * cap : (m + 1) * cap] * slot_mask, axis=0, keepdims=True
        )

    owner_hot = as_bf16((slot_row >> cap_bits) == iota((dp, rows), 0))
    slot_hot = as_f32((slot_row & (cap - 1)) == iota((cap, rows), 0))
    label_row = labels[...].astype(F32)
    zeros_row = jnp.zeros((LANES - 2 * cap, rows), BF16)

    def wait_all(ref, sem):
        pltpu.make_async_copy(ref, ref, sem).wait()

    wait_all(recv_p.at[pl.ds(0, feat - 1)], rp)
    fixed_score = recv_p[0]
    for k in range(1, feat):
        fixed_score = fixed_score + recv_p[k]

    sent = fixed_score.astype(BF16).astype(F32)
    payload = jnp.concatenate(
        [(slot_hot * sent).astype(BF16), (slot_hot * label_row).astype(BF16), zeros_row], axis=0
    )
    scattered = dot_nt(owner_hot, payload)
    send_s[...] = scattered.reshape(dp, 1, LANES)

    def send_score(k, carry):
        owner = (i + k) % dp
        pltpu.make_async_remote_copy(
            src_ref=send_s.at[owner],
            dst_ref=recv_s.at[i],
            send_sem=ss,
            recv_sem=rs,
            device_id=at(owner),
            device_id_type=MESH,
        ).start()
        return carry

    lax.fori_loop(1, dp, send_score, 0)
    recv_s[i] = send_s[i]
    wait_all(recv_x.at[pl.ds(0, dp - 1)], rx)
    wait_all(recv_s.at[pl.ds(0, dp - 1)], rs)

    mask = member_mask[...]
    got = recv_x[...].reshape(slots, feats.shape[1])
    arrived = recv_s[...].reshape(dp, LANES)[:, : 2 * cap].astype(BF16)
    expanded = dot_tn(arrived, spread)
    score_row = jnp.sum(expanded[:cap] * slot_mask, axis=0, keepdims=True)
    answer_row = jnp.sum(expanded[cap:] * slot_mask, axis=0, keepdims=True)

    def project(vectors):
        top, low = split2(vectors)
        dots = dot_nt(jnp.concatenate([top, low], axis=0), got)
        return jnp.sum((dots[:members] + dots[members:]) * mask, axis=0, keepdims=True)

    def gather_rows(weights):
        top, low = split2(mask * weights)
        sums = dot_nn(jnp.concatenate([top, low], axis=0), got)
        return sums[:members] + sums[members:]

    coef = mcoef[...]
    probability = 1.0 / (1.0 + jnp.exp(-(score_row + project(coef))))
    weight = probability * (1.0 - probability)
    gradient = gather_rows(answer_row - probability) - RIDGE_MEMBER * coef
    got_wide = got.astype(F32)
    square_top, square_low = split2(got_wide * got_wide)
    weight_top, weight_low = split2(mask * weight)
    first = dot_nn(jnp.concatenate([weight_top, weight_low], axis=0), square_top)
    second = dot_nn(weight_top, square_low)
    diagonal = first[:members] + first[members:] + second + RIDGE_MEMBER
    step_sum = jnp.zeros_like(coef)
    remain = gradient
    scaled = remain / diagonal
    search = scaled
    inner_product = jnp.sum(remain * scaled, axis=1, keepdims=True)
    for iteration in range(CG_ITERS):
        image = gather_rows(weight * project(search)) + RIDGE_MEMBER * search
        alpha = inner_product / jnp.sum(search * image, axis=1, keepdims=True)
        step_sum = step_sum + alpha * search
        if iteration + 1 < CG_ITERS:
            remain = remain - alpha * image
            scaled = remain / diagonal
            inner_next = jnp.sum(remain * scaled, axis=1, keepdims=True)
            search = scaled + (inner_next / inner_product) * search
            inner_product = inner_next
    updated = coef + step_sum
    coef_out[...] = updated

    new_top, new_low = split2(project(updated))
    stacked = jnp.concatenate([spread * new_top, spread * new_low], axis=0)
    slot_wide = as_bf16((iota((LANES, slots), 1) & (cap - 1)) == iota((LANES, slots), 0))
    folded = dot_nt(stacked, slot_wide)
    send_r[...] = (folded[:dp] + folded[dp:]).reshape(dp, 1, LANES)

    def send_back(k, carry):
        sender = (i + k) % dp
        pltpu.make_async_remote_copy(
            src_ref=send_r.at[sender],
            dst_ref=recv_r.at[i],
            send_sem=sr,
            recv_sem=rr,
            device_id=at(sender),
            device_id_type=MESH,
        ).start()
        return carry

    lax.fori_loop(1, dp, send_back, 0)
    recv_r[i] = send_r[i]
    wait_all(recv_r.at[pl.ds(0, dp - 1)], rr)
    back_top, back_low = split2(recv_r[...].reshape(dp, LANES)[:, :cap])
    looked = dot_tn(back_top, owner_hot) + dot_tn(back_low, owner_hot)
    member_score = jnp.sum(looked * slot_hot, axis=0, keepdims=True)
    margin = fixed_score + member_score
    margin_out[...] = margin
    send_e[...] = label_row - 1.0 / (1.0 + jnp.exp(-margin))
    for k in range(1, feat):
        other = (f + k) % feat
        pltpu.make_async_remote_copy(
            src_ref=send_e,
            dst_ref=recv_e.at[f],
            send_sem=se.at[k - 1],
            recv_sem=re,
            device_id=at(i, other),
            device_id_type=MESH,
        ).start()
    recv_e[f] = send_e[...]
    wait_all(recv_e.at[pl.ds(0, feat - 1)], re)

    half = block_count // cores
    piece = half // 2

    def gradient_rows(start):
        def add_chunk(q, total):
            first_row = pl.multiple_of(q * step, step)
            values = fv[pl.ds(first_row, step), :]
            per = rows // step
            inner = pl.multiple_of((q % per) * step, step)
            left = recv_e[q // per, :, pl.ds(inner, step)]
            hot = fb[:, pl.ds(first_row, step)] - start == iota((piece, step), 0)
            weighted = jnp.where(hot, left, 0.0)
            top, low = split2(weighted)
            return total + dot_nn(top, values) + dot_nn(low, values)

        acc[pl.ds(start, piece), :] = lax.fori_loop(
            0, group_rows // step, add_chunk, jnp.zeros((piece, block_width), F32)
        )

    partner = z * plane_owners + x * cores + (1 - c)
    theirs = (1 - c) * half
    core_copies = []
    for k in range(2):
        start = pl.multiple_of(theirs + k * piece, piece)
        gradient_rows(start)
        copy = pltpu.make_async_remote_copy(
            src_ref=acc.at[pl.ds(start, piece)],
            dst_ref=recv_c.at[pl.ds(k * piece, piece)],
            send_sem=sc.at[k],
            recv_sem=rc.at[k],
            device_id=at(partner),
            device_id_type=MESH,
        )
        copy.start()
        core_copies.append(copy)
    mine = pl.multiple_of(c * half, half)
    for k in range(2):
        gradient_rows(pl.multiple_of(mine + k * piece, piece))
    for copy in core_copies:
        copy.wait_recv()
    acc[pl.ds(mine, half), :] = acc[pl.ds(mine, half), :] + recv_c[...]

    strip = half // chips
    share = strip // planes

    def along_x(k):
        return (x + k) % chips

    def along_z(k):
        return (z + k) % planes

    for k in range(1, chips):
        other = along_x(k)
        pltpu.make_async_remote_copy(
            src_ref=acc.at[pl.ds(pl.multiple_of(mine + other * strip, strip), strip)],
            dst_ref=recv_rx.at[x],
            send_sem=srx,
            recv_sem=rrx,
            device_id=at(z * plane_owners + other * cores + c),
            device_id_type=MESH,
        ).start()
    my_strip = pl.multiple_of(mine + x * strip, strip)
    recv_rx[x] = acc[pl.ds(my_strip, strip), :]
    wait_all(recv_rx.at[pl.ds(0, chips - 1)], rrx)
    total = recv_rx[0]
    for k in range(1, chips):
        total = total + recv_rx[k]
    acc[pl.ds(my_strip, strip), :] = total
    for k in range(1, planes):
        other = along_z(k)
        pltpu.make_async_remote_copy(
            src_ref=acc.at[pl.ds(pl.multiple_of(my_strip + other * share, share), share)],
            dst_ref=recv_rz.at[z],
            send_sem=srz,
            recv_sem=rrz,
            device_id=at(other * plane_owners + x * cores + c),
            device_id_type=MESH,
        ).start()
    my_share = pl.multiple_of(my_strip + z * share, share)
    recv_rz[z] = acc[pl.ds(my_share, share), :]
    wait_all(recv_rz.at[pl.ds(0, planes - 1)], rrz)
    total = recv_rz[0]
    for k in range(1, planes):
        total = total + recv_rz[k]
    grad_out[pl.ds(my_share, share), :] = (
        RIDGE_FIXED * fc[pl.ds(my_share, share), :] - total / dp
    )

    for k in range(1, planes):
        pltpu.make_async_remote_copy(
            src_ref=grad_out.at[pl.ds(my_share, share)],
            dst_ref=grad_out.at[pl.ds(my_share, share)],
            send_sem=sgz,
            recv_sem=rgz,
            device_id=at(along_z(k) * plane_owners + x * cores + c),
            device_id_type=MESH,
        ).start()
    wait_all(grad_out.at[pl.ds(0, (planes - 1) * share)], rgz)
    for k in range(1, chips):
        pltpu.make_async_remote_copy(
            src_ref=grad_out.at[pl.ds(my_strip, strip)],
            dst_ref=grad_out.at[pl.ds(my_strip, strip)],
            send_sem=sgx,
            recv_sem=rgx,
            device_id=at(z * plane_owners + along_x(k) * cores + c),
            device_id_type=MESH,
        ).start()
    wait_all(grad_out.at[pl.ds(0, (chips - 1) * strip)], rgx)
    last = pltpu.make_async_remote_copy(
        src_ref=grad_out.at[pl.ds(mine, half)],
        dst_ref=grad_out.at[pl.ds(mine, half)],
        send_sem=sgc,
        recv_sem=rgc,
        device_id=at(partner),
        device_id_type=MESH,
    )
    last.start()
    last.wait()

    wait_all(send_x.at[pl.ds(0, dp - 1)], sx)
    wait_all(send_p.at[pl.ds(0, feat - 1)], sp)
    wait_all(send_s.at[pl.ds(0, dp - 1)], ss)
    wait_all(send_r.at[pl.ds(0, dp - 1)], sr)
    for k in range(1, feat):
        wait_all(send_e, se.at[k - 1])
    for copy in core_copies:
        copy.wait_send()
    wait_all(recv_rx.at[pl.ds(0, chips - 1)], srx)
    wait_all(recv_rz.at[pl.ds(0, planes - 1)], srz)
    wait_all(grad_out.at[pl.ds(0, (planes - 1) * share)], sgz)
    wait_all(grad_out.at[pl.ds(0, (chips - 1) * strip)], sgx)


def body(
    member_feats,
    labels,
    fixed_values,
    fixed_blocks,
    fixed_coef,
    member_coef,
    row_slot,
    tile_source,
    member_tiles,
):
    dp = lax.axis_size("dp")
    feat = lax.axis_size("feat")
    planes, chips, cores = grid_of(dp)
    rows, width = member_feats.shape
    members = member_coef.shape[0]
    block_count, block_width = fixed_coef.shape
    cap = 2 * rows // dp
    half = block_count // cores
    vmem = pl.BlockSpec(memory_space=pltpu.VMEM)
    smem = pl.BlockSpec(memory_space=pltpu.SMEM)
    dma = pltpu.SemaphoreType.DMA
    margin, updated, grad = pl.pallas_call(
        functools.partial(kernel, dp, feat, cap),
        out_shape=(
            jax.ShapeDtypeStruct((1, rows), F32),
            jax.ShapeDtypeStruct((members, width), F32),
            jax.ShapeDtypeStruct((block_count, block_width), F32),
        ),
        in_specs=[vmem] * 8 + [smem],
        out_specs=(vmem, vmem, vmem),
        scratch_shapes=[
            pltpu.VMEM((dp, cap, width), BF16),
            pltpu.VMEM((dp, cap, width), BF16),
            pltpu.VMEM((feat, 1, rows), F32),
            pltpu.VMEM((feat, 1, rows), F32),
            pltpu.VMEM((dp, 1, LANES), F32),
            pltpu.VMEM((dp, 1, LANES), F32),
            pltpu.VMEM((dp, 1, LANES), F32),
            pltpu.VMEM((dp, 1, LANES), F32),
            pltpu.VMEM((1, rows), F32),
            pltpu.VMEM((feat, 1, rows), F32),
            pltpu.VMEM((2, block_count, block_width), BF16),
            pltpu.VMEM((members, dp * cap), F32),
            pltpu.VMEM((block_count, block_width), F32),
            pltpu.VMEM((half, block_width), F32),
            pltpu.VMEM((chips, half // chips, block_width), F32),
            pltpu.VMEM((planes, half // chips // planes, block_width), F32),
            dma,
            dma,
            dma,
            dma,
            dma,
            dma,
            dma,
            dma,
            dma((feat - 1,)),
            dma,
            dma((2,)),
            dma((2,)),
            dma,
            dma,
            dma,
            dma,
            dma,
            dma,
            dma,
            dma,
            dma,
            dma,
        ],
        compiler_params=pltpu.CompilerParams(
            collective_id=0, has_side_effects=True, vmem_limit_bytes=56 * 2**20
        ),
    )(
        member_feats,
        labels.reshape(1, rows),
        fixed_values,
        fixed_blocks.reshape(1, feat * rows),
        fixed_coef,
        member_coef,
        row_slot.reshape(1, rows),
        tile_source.reshape(1, -1),
        member_tiles,
    )
    return margin.reshape(rows), updated, grad


def solution(mesh):
    placed = (
        P(("dp", "feat"), None),
        P(("dp", "feat")),
        P("dp", "feat"),
        P("dp", "feat"),
        P("feat", None),
        P(("dp", "feat"), None),
        P(("dp", "feat")),
        P(("dp", "feat")),
        P(("dp", "feat")),
    )
    return jax.shard_map(
        body,
        mesh=mesh,
        in_specs=placed,
        out_specs=(P(("dp", "feat")), P(("dp", "feat"), None), P("feat", None)),
        check_vma=False,
    )
```

```python
import functools

import jax
import jax.numpy as jnp
from jax import lax
from jax.experimental import pallas as pl
from jax.experimental.pallas import tpu as pltpu
from jax.sharding import PartitionSpec as P

CG_ITERS = 2
TILE = 128
LANES = 128
RIDGE_MEMBER = 1.0
RIDGE_FIXED = 1.0
F32 = jnp.float32
BF16 = jnp.bfloat16
MESH = pl.DeviceIdType.MESH


def dot_nn(a, b):
    return lax.dot_general(a, b, (((1,), (0,)), ((), ())), preferred_element_type=F32)


def dot_nt(a, b):
    return lax.dot_general(a, b, (((1,), (1,)), ((), ())), preferred_element_type=F32)


def dot_tn(a, b):
    return lax.dot_general(a, b, (((0,), (0,)), ((), ())), preferred_element_type=F32)


def split2(x):
    top = x.astype(BF16)
    return top, (x - top.astype(F32)).astype(BF16)


def iota(shape, dim):
    return lax.broadcasted_iota(jnp.int32, shape, dim)


def as_bf16(mask):
    return jnp.where(mask, 1.0, 0.0).astype(BF16)


def as_f32(mask):
    return jnp.where(mask, 1.0, 0.0).astype(F32)


def grid_of(dp):
    return (8, 4, 2) if dp == 64 else (dp // 4, 2, 2)


def kernel(
    dp,
    feat,
    cap,
    feats_hbm,
    labels,
    fv_hbm,
    fb,
    fc_hbm,
    mcoef,
    rslot,
    tsrc,
    mtiles,
    margin_out,
    coef_out,
    grad_out,
    feats,
    fv,
    fc,
    hot_all,
    send_x,
    recv_x,
    send_p,
    recv_p,
    send_s,
    recv_s,
    send_r,
    recv_r,
    send_e,
    recv_e,
    coef_parts,
    member_mask,
    acc,
    recv_c,
    recv_rx,
    recv_rz,
    sx,
    rx,
    sp,
    rp,
    ss,
    rs,
    sr,
    rr,
    se,
    re,
    sc,
    rc,
    srx,
    rrx,
    srz,
    rrz,
    sgz,
    rgz,
    sgx,
    rgx,
    sgc,
    rgc,
    s_load,
):
    planes, chips, cores = grid_of(dp)
    rows = feats.shape[0]
    slots = dp * cap
    cap_bits = cap.bit_length() - 1
    block_count, block_width = fc.shape
    plane_owners = chips * cores
    plane_slots = plane_owners * cap
    i = lax.axis_index("dp")
    f = lax.axis_index("feat")
    z = i // plane_owners
    x = (i % plane_owners) // cores
    c = i % cores

    def at(dp_index, feat_index=None):
        return (dp_index, f if feat_index is None else feat_index)

    def wait_all(ref, sem):
        pltpu.make_async_copy(ref, ref, sem).wait()

    loads = [
        pltpu.make_async_copy(source, target, s_load.at[k])
        for k, (source, target) in enumerate(((feats_hbm, feats), (fc_hbm, fc), (fv_hbm, fv)))
    ]
    for load in loads:
        load.start()

    barrier = pltpu.get_barrier_semaphore()

    def greet_dp(k, carry):
        pl.semaphore_signal(barrier, inc=1, device_id=at((i + k) % dp), device_id_type=MESH)
        return carry

    lax.fori_loop(1, dp, greet_dp, 0)
    for k in range(1, feat):
        pl.semaphore_signal(
            barrier, inc=1, device_id=at(i, (f + k) % feat), device_id_type=MESH
        )

    slot_row = rslot[...]
    loads[0].wait()
    feats_here = feats[...]

    def pick_plane(plane, carry):
        base = plane * plane_slots
        pick = as_bf16(slot_row - base == iota((plane_slots, rows), 0))
        picked = dot_nn(pick, feats_here).astype(BF16)
        send_x[pl.ds(plane * plane_owners, plane_owners)] = picked.reshape(
            plane_owners, cap, feats.shape[1]
        )
        return carry

    lax.fori_loop(0, planes, pick_plane, 0)
    pl.semaphore_wait(barrier, dp - 1 + feat - 1)

    def send_feats(owner):
        pltpu.make_async_remote_copy(
            src_ref=send_x.at[owner],
            dst_ref=recv_x.at[i],
            send_sem=sx,
            recv_sem=rx,
            device_id=at(owner),
            device_id_type=MESH,
        ).start()

    def send_far(q, carry):
        for k in sorted(range(1, planes), key=lambda k: -min(k, planes - k)):
            send_feats(((z + k) % planes) * plane_owners + (i + q) % plane_owners)
        return carry

    def send_near(q, carry):
        send_feats(z * plane_owners + (i + q) % plane_owners)
        return carry

    lax.fori_loop(0, plane_owners, send_far, 0)
    lax.fori_loop(1, plane_owners, send_near, 0)
    recv_x[i] = send_x[i]

    group_rows = feat * rows
    step = min(512, rows)
    loads[1].wait()
    coef_top, coef_low = split2(fc[...])
    coef_parts[:block_count] = coef_top
    coef_parts[block_count:] = coef_low
    loads[2].wait()

    def partial_chunk(q, carry):
        start = pl.multiple_of(q * step, step)
        values = fv[pl.ds(start, step), :]
        scores = dot_nt(coef_parts[...], values)
        scores = scores[:block_count] + scores[block_count:]
        hot = as_f32(fb[:, pl.ds(start, step)] == iota((block_count, step), 0))
        hot_all[:, pl.ds(start, step)] = hot.astype(BF16)
        part = jnp.sum(scores * hot, axis=0, keepdims=True)
        per = rows // step
        inner = pl.multiple_of((q % per) * step, step)
        send_p[q // per, :, pl.ds(inner, step)] = part
        return carry

    lax.fori_loop(0, group_rows // step, partial_chunk, 0)
    for k in range(1, feat):
        other = (f + k) % feat
        pltpu.make_async_remote_copy(
            src_ref=send_p.at[other],
            dst_ref=recv_p.at[f],
            send_sem=sp,
            recv_sem=rp,
            device_id=at(i, other),
            device_id_type=MESH,
        ).start()
    recv_p[f] = send_p[f]

    positions = tsrc.shape[0]
    tile = iota((1, positions), 1) >> (TILE.bit_length() - 1)
    members = mcoef.shape[0]
    member = jnp.zeros((1, positions), jnp.int32)
    end = jnp.int32(0)
    for m in range(members):
        end = end + mtiles[m]
        member = member + jnp.where(tile >= end, 1, 0)
    source = tsrc[...].reshape(1, positions)
    code = (member << cap_bits) + (source & (cap - 1))
    code_hot = as_bf16(code == iota((members * cap, positions), 0))
    sender_hot = as_bf16((source >> cap_bits) == iota((dp, positions), 0))
    counted = dot_nt(code_hot, sender_hot).astype(BF16)
    spread = as_bf16((iota((dp, slots), 1) >> cap_bits) == iota((dp, slots), 0))
    slot_mask = as_f32((iota((cap, slots), 1) & (cap - 1)) == iota((cap, slots), 0))
    widened = dot_nn(counted, spread)
    for m in range(members):
        member_mask[pl.ds(m, 1), :] = jnp.sum(
            widened[m * cap : (m + 1) * cap] * slot_mask, axis=0, keepdims=True
        )

    owner_hot = as_bf16((slot_row >> cap_bits) == iota((dp, rows), 0))
    slot_hot = as_f32((slot_row & (cap - 1)) == iota((cap, rows), 0))
    label_row = labels[...].astype(F32)
    zeros_row = jnp.zeros((LANES - 2 * cap, rows), BF16)

    wait_all(recv_p.at[pl.ds(0, feat - 1)], rp)
    fixed_score = recv_p[0]
    for k in range(1, feat):
        fixed_score = fixed_score + recv_p[k]

    sent = fixed_score.astype(BF16).astype(F32)
    payload = jnp.concatenate(
        [(slot_hot * sent).astype(BF16), (slot_hot * label_row).astype(BF16), zeros_row], axis=0
    )
    scattered = dot_nt(owner_hot, payload)
    send_s[...] = scattered.reshape(dp, 1, LANES)

    def send_score(k, carry):
        owner = (i + k) % dp
        pltpu.make_async_remote_copy(
            src_ref=send_s.at[owner],
            dst_ref=recv_s.at[i],
            send_sem=ss,
            recv_sem=rs,
            device_id=at(owner),
            device_id_type=MESH,
        ).start()
        return carry

    lax.fori_loop(1, dp, send_score, 0)
    recv_s[i] = send_s[i]
    wait_all(recv_x.at[pl.ds(0, dp - 1)], rx)
    wait_all(recv_s.at[pl.ds(0, dp - 1)], rs)

    mask = member_mask[...]
    got = recv_x[...].reshape(slots, feats.shape[1])
    arrived = recv_s[...].reshape(dp, LANES)[:, : 2 * cap].astype(BF16)
    expanded = dot_tn(arrived, spread)
    score_row = jnp.sum(expanded[:cap] * slot_mask, axis=0, keepdims=True)
    answer_row = jnp.sum(expanded[cap:] * slot_mask, axis=0, keepdims=True)

    def project(vectors):
        top, low = split2(vectors)
        dots = dot_nt(jnp.concatenate([top, low], axis=0), got)
        return jnp.sum((dots[:members] + dots[members:]) * mask, axis=0, keepdims=True)

    def gather_rows(weights):
        top, low = split2(mask * weights)
        sums = dot_nn(jnp.concatenate([top, low], axis=0), got)
        return sums[:members] + sums[members:]

    coef = mcoef[...]
    probability = 1.0 / (1.0 + jnp.exp(-(score_row + project(coef))))
    weight = probability * (1.0 - probability)
    gradient = gather_rows(answer_row - probability) - RIDGE_MEMBER * coef
    got_wide = got.astype(F32)
    square_top, square_low = split2(got_wide * got_wide)
    weight_top, weight_low = split2(mask * weight)
    first = dot_nn(jnp.concatenate([weight_top, weight_low], axis=0), square_top)
    second = dot_nn(weight_top, square_low)
    diagonal = first[:members] + first[members:] + second + RIDGE_MEMBER
    step_sum = jnp.zeros_like(coef)
    remain = gradient
    scaled = remain / diagonal
    search = scaled
    inner_product = jnp.sum(remain * scaled, axis=1, keepdims=True)
    for iteration in range(CG_ITERS):
        image = gather_rows(weight * project(search)) + RIDGE_MEMBER * search
        alpha = inner_product / jnp.sum(search * image, axis=1, keepdims=True)
        step_sum = step_sum + alpha * search
        if iteration + 1 < CG_ITERS:
            remain = remain - alpha * image
            scaled = remain / diagonal
            inner_next = jnp.sum(remain * scaled, axis=1, keepdims=True)
            search = scaled + (inner_next / inner_product) * search
            inner_product = inner_next
    updated = coef + step_sum
    coef_out[...] = updated

    new_top, new_low = split2(project(updated))
    stacked = jnp.concatenate([spread * new_top, spread * new_low], axis=0)
    slot_wide = as_bf16((iota((LANES, slots), 1) & (cap - 1)) == iota((LANES, slots), 0))
    folded = dot_nt(stacked, slot_wide)
    send_r[...] = (folded[:dp] + folded[dp:]).reshape(dp, 1, LANES)

    def send_back(k, carry):
        sender = (i + k) % dp
        pltpu.make_async_remote_copy(
            src_ref=send_r.at[sender],
            dst_ref=recv_r.at[i],
            send_sem=sr,
            recv_sem=rr,
            device_id=at(sender),
            device_id_type=MESH,
        ).start()
        return carry

    lax.fori_loop(1, dp, send_back, 0)
    recv_r[i] = send_r[i]
    wait_all(recv_r.at[pl.ds(0, dp - 1)], rr)
    back_top, back_low = split2(recv_r[...].reshape(dp, LANES)[:, :cap])
    looked = dot_tn(back_top, owner_hot) + dot_tn(back_low, owner_hot)
    member_score = jnp.sum(looked * slot_hot, axis=0, keepdims=True)
    margin = fixed_score + member_score
    margin_out[...] = margin
    send_e[...] = label_row - 1.0 / (1.0 + jnp.exp(-margin))
    for k in range(1, feat):
        other = (f + k) % feat
        pltpu.make_async_remote_copy(
            src_ref=send_e,
            dst_ref=recv_e.at[f],
            send_sem=se.at[k - 1],
            recv_sem=re,
            device_id=at(i, other),
            device_id_type=MESH,
        ).start()
    recv_e[f] = send_e[...]
    wait_all(recv_e.at[pl.ds(0, feat - 1)], re)

    half = block_count // cores

    def gradient_rows(start):
        def add_chunk(q, total):
            first_row = pl.multiple_of(q * step, step)
            per = rows // step
            inner = pl.multiple_of((q % per) * step, step)
            top, low = split2(recv_e[q // per, :, pl.ds(inner, step)])
            hot = hot_all[pl.ds(start, half), pl.ds(first_row, step)]
            weighted = jnp.concatenate([hot * top, hot * low], axis=0)
            return total + dot_nn(weighted, fv[pl.ds(first_row, step), :])

        total = lax.fori_loop(
            0, group_rows // step, add_chunk, jnp.zeros((2 * half, block_width), F32)
        )
        acc[pl.ds(start, half), :] = total[:half] + total[half:]

    partner = z * plane_owners + x * cores + (1 - c)
    theirs = pl.multiple_of((1 - c) * half, half)
    mine = pl.multiple_of(c * half, half)
    gradient_rows(theirs)
    core_copy = pltpu.make_async_remote_copy(
        src_ref=acc.at[pl.ds(theirs, half)],
        dst_ref=recv_c,
        send_sem=sc,
        recv_sem=rc,
        device_id=at(partner),
        device_id_type=MESH,
    )
    core_copy.start()
    gradient_rows(mine)
    core_copy.wait_recv()
    acc[pl.ds(mine, half), :] = acc[pl.ds(mine, half), :] + recv_c[...]

    strip = half // chips
    share = strip // planes

    def along_x(k):
        return (x + k) % chips

    def along_z(k):
        return (z + k) % planes

    for k in range(1, chips):
        other = along_x(k)
        pltpu.make_async_remote_copy(
            src_ref=acc.at[pl.ds(pl.multiple_of(mine + other * strip, strip), strip)],
            dst_ref=recv_rx.at[x],
            send_sem=srx,
            recv_sem=rrx,
            device_id=at(z * plane_owners + other * cores + c),
            device_id_type=MESH,
        ).start()
    my_strip = pl.multiple_of(mine + x * strip, strip)
    recv_rx[x] = acc[pl.ds(my_strip, strip), :]
    wait_all(recv_rx.at[pl.ds(0, chips - 1)], rrx)
    total = recv_rx[0]
    for k in range(1, chips):
        total = total + recv_rx[k]
    acc[pl.ds(my_strip, strip), :] = total
    for k in range(1, planes):
        other = along_z(k)
        pltpu.make_async_remote_copy(
            src_ref=acc.at[pl.ds(pl.multiple_of(my_strip + other * share, share), share)],
            dst_ref=recv_rz.at[z],
            send_sem=srz,
            recv_sem=rrz,
            device_id=at(other * plane_owners + x * cores + c),
            device_id_type=MESH,
        ).start()
    my_share = pl.multiple_of(my_strip + z * share, share)
    recv_rz[z] = acc[pl.ds(my_share, share), :]
    wait_all(recv_rz.at[pl.ds(0, planes - 1)], rrz)
    total = recv_rz[0]
    for k in range(1, planes):
        total = total + recv_rz[k]
    grad_out[pl.ds(my_share, share), :] = (
        RIDGE_FIXED * fc[pl.ds(my_share, share), :] - total / dp
    )

    for k in range(1, planes):
        pltpu.make_async_remote_copy(
            src_ref=grad_out.at[pl.ds(my_share, share)],
            dst_ref=grad_out.at[pl.ds(my_share, share)],
            send_sem=sgz,
            recv_sem=rgz,
            device_id=at(along_z(k) * plane_owners + x * cores + c),
            device_id_type=MESH,
        ).start()
    wait_all(grad_out.at[pl.ds(0, (planes - 1) * share)], rgz)
    for k in range(1, chips):
        pltpu.make_async_remote_copy(
            src_ref=grad_out.at[pl.ds(my_strip, strip)],
            dst_ref=grad_out.at[pl.ds(my_strip, strip)],
            send_sem=sgx,
            recv_sem=rgx,
            device_id=at(z * plane_owners + along_x(k) * cores + c),
            device_id_type=MESH,
        ).start()
    wait_all(grad_out.at[pl.ds(0, (chips - 1) * strip)], rgx)
    last = pltpu.make_async_remote_copy(
        src_ref=grad_out.at[pl.ds(mine, half)],
        dst_ref=grad_out.at[pl.ds(mine, half)],
        send_sem=sgc,
        recv_sem=rgc,
        device_id=at(partner),
        device_id_type=MESH,
    )
    last.start()
    last.wait()

    wait_all(send_x.at[pl.ds(0, dp - 1)], sx)
    wait_all(send_p.at[pl.ds(0, feat - 1)], sp)
    wait_all(send_s.at[pl.ds(0, dp - 1)], ss)
    wait_all(send_r.at[pl.ds(0, dp - 1)], sr)
    for k in range(1, feat):
        wait_all(send_e, se.at[k - 1])
    core_copy.wait_send()
    wait_all(recv_rx.at[pl.ds(0, chips - 1)], srx)
    wait_all(recv_rz.at[pl.ds(0, planes - 1)], srz)
    wait_all(grad_out.at[pl.ds(0, (planes - 1) * share)], sgz)
    wait_all(grad_out.at[pl.ds(0, (chips - 1) * strip)], sgx)


def hand_over(margin, updated, grad, margin_out, updated_out, grad_out, sems):
    copies = [
        pltpu.make_async_copy(source, target, sems.at[k])
        for k, (source, target) in enumerate(
            ((grad, grad_out), (updated, updated_out), (margin, margin_out))
        )
    ]
    for copy in copies:
        copy.start()
    for copy in copies:
        copy.wait()


def body(
    member_feats,
    labels,
    fixed_values,
    fixed_blocks,
    fixed_coef,
    member_coef,
    row_slot,
    tile_source,
    member_tiles,
):
    dp = lax.axis_size("dp")
    feat = lax.axis_size("feat")
    planes, chips, cores = grid_of(dp)
    rows, width = member_feats.shape
    members = member_coef.shape[0]
    block_count, block_width = fixed_coef.shape
    cap = 2 * rows // dp
    half = block_count // cores
    vmem = pl.BlockSpec(memory_space=pltpu.VMEM)
    hbm = pl.BlockSpec(memory_space=pl.ANY)
    smem = pl.BlockSpec(memory_space=pltpu.SMEM)
    dma = pltpu.SemaphoreType.DMA
    margin, updated, grad = pl.pallas_call(
        functools.partial(kernel, dp, feat, cap),
        out_shape=(
            jax.ShapeDtypeStruct((1, rows), F32),
            jax.ShapeDtypeStruct((members, width), F32),
            jax.ShapeDtypeStruct((block_count, block_width), F32),
        ),
        in_specs=[hbm, vmem, hbm, vmem, hbm, vmem, vmem, vmem, smem],
        out_specs=(vmem, vmem, vmem),
        scratch_shapes=[
            pltpu.VMEM((rows, width), BF16),
            pltpu.VMEM(fixed_values.shape, BF16),
            pltpu.VMEM((block_count, block_width), F32),
            pltpu.VMEM((block_count, feat * rows), BF16),
            pltpu.VMEM((dp, cap, width), BF16),
            pltpu.VMEM((dp, cap, width), BF16),
            pltpu.VMEM((feat, 1, rows), F32),
            pltpu.VMEM((feat, 1, rows), F32),
            pltpu.VMEM((dp, 1, LANES), F32),
            pltpu.VMEM((dp, 1, LANES), F32),
            pltpu.VMEM((dp, 1, LANES), F32),
            pltpu.VMEM((dp, 1, LANES), F32),
            pltpu.VMEM((1, rows), F32),
            pltpu.VMEM((feat, 1, rows), F32),
            pltpu.VMEM((2 * block_count, block_width), BF16),
            pltpu.VMEM((members, dp * cap), F32),
            pltpu.VMEM((block_count, block_width), F32),
            pltpu.VMEM((half, block_width), F32),
            pltpu.VMEM((chips, half // chips, block_width), F32),
            pltpu.VMEM((planes, half // chips // planes, block_width), F32),
            dma,
            dma,
            dma,
            dma,
            dma,
            dma,
            dma,
            dma,
            dma((feat - 1,)),
            dma,
            dma,
            dma,
            dma,
            dma,
            dma,
            dma,
            dma,
            dma,
            dma,
            dma,
            dma,
            dma,
            dma((3,)),
        ],
        compiler_params=pltpu.CompilerParams(
            collective_id=0, has_side_effects=True, vmem_limit_bytes=56 * 2**20
        ),
    )(
        member_feats,
        labels.reshape(1, rows),
        fixed_values,
        fixed_blocks.reshape(1, feat * rows),
        fixed_coef,
        member_coef,
        row_slot.reshape(1, rows),
        tile_source,
        member_tiles,
    )
    margin, updated, grad = pl.pallas_call(
        hand_over,
        out_shape=(
            jax.ShapeDtypeStruct((1, rows), F32),
            jax.ShapeDtypeStruct((members, width), F32),
            jax.ShapeDtypeStruct((block_count, block_width), F32),
        ),
        in_specs=[hbm] * 3,
        out_specs=(hbm,) * 3,
        scratch_shapes=[dma((3,))],
    )(margin, updated, grad)
    return margin.reshape(rows), updated, grad


def solution(mesh):
    placed = (
        P(("dp", "feat"), None),
        P(("dp", "feat")),
        P("dp", "feat"),
        P("dp", "feat"),
        P("feat", None),
        P(("dp", "feat"), None),
        P(("dp", "feat")),
        P(("dp", "feat")),
        P(("dp", "feat")),
    )
    return jax.shard_map(
        body,
        mesh=mesh,
        in_specs=placed,
        out_specs=(P(("dp", "feat")), P(("dp", "feat"), None), P("feat", None)),
        check_vma=False,
    )
```

```python
import functools

import jax
import jax.numpy as jnp
from jax import lax
from jax.experimental import pallas as pl
from jax.experimental.pallas import tpu as pltpu
from jax.sharding import PartitionSpec as P

CG_ITERS = 2
TILE = 128
LANES = 128
RIDGE_MEMBER = 1.0
RIDGE_FIXED = 1.0
F32 = jnp.float32
BF16 = jnp.bfloat16
MESH = pl.DeviceIdType.MESH


def dot_nn(a, b):
    return lax.dot_general(a, b, (((1,), (0,)), ((), ())), preferred_element_type=F32)


def dot_nt(a, b):
    return lax.dot_general(a, b, (((1,), (1,)), ((), ())), preferred_element_type=F32)


def dot_tn(a, b):
    return lax.dot_general(a, b, (((0,), (0,)), ((), ())), preferred_element_type=F32)


def split2(x):
    top = x.astype(BF16)
    return top, (x - top.astype(F32)).astype(BF16)


def iota(shape, dim):
    return lax.broadcasted_iota(jnp.int32, shape, dim)


def as_bf16(mask):
    return jnp.where(mask, 1.0, 0.0).astype(BF16)


def as_f32(mask):
    return jnp.where(mask, 1.0, 0.0).astype(F32)


def grid_of(dp):
    return (8, 4, 2) if dp == 64 else (dp // 4, 2, 2)


def kernel(
    dp,
    feat,
    cap,
    feats_hbm,
    labels,
    fv_hbm,
    fb,
    fc_hbm,
    mcoef,
    rslot,
    tsrc,
    mtiles,
    margin_out,
    coef_out,
    grad_out,
    feats,
    fv,
    fc,
    hot_all,
    send_x,
    recv_x,
    send_p,
    recv_p,
    send_s,
    recv_s,
    send_r,
    recv_r,
    send_e,
    recv_e,
    coef_parts,
    member_mask,
    acc,
    recv_c,
    send_q,
    recv_q,
    full_q,
    send_k,
    recv_k,
    full_k,
    sx,
    rx,
    sp,
    rp,
    ss,
    rs,
    sr,
    rr,
    se,
    re,
    sc,
    rc,
    sq,
    rq,
    sg,
    rg,
    sgc,
    rgc,
    s_load,
):
    planes, chips, cores = grid_of(dp)
    rows = feats.shape[0]
    slots = dp * cap
    cap_bits = cap.bit_length() - 1
    block_count, block_width = fc.shape
    plane_owners = chips * cores
    plane_slots = plane_owners * cap
    i = lax.axis_index("dp")
    f = lax.axis_index("feat")
    z = i // plane_owners
    x = (i % plane_owners) // cores
    c = i % cores

    def at(dp_index, feat_index=None):
        return (dp_index, f if feat_index is None else feat_index)

    def wait_all(ref, sem):
        pltpu.make_async_copy(ref, ref, sem).wait()

    loads = [
        pltpu.make_async_copy(source, target, s_load.at[k])
        for k, (source, target) in enumerate(((feats_hbm, feats), (fc_hbm, fc), (fv_hbm, fv)))
    ]
    for load in loads:
        load.start()

    barrier = pltpu.get_barrier_semaphore()

    def greet_dp(k, carry):
        pl.semaphore_signal(barrier, inc=1, device_id=at((i + k) % dp), device_id_type=MESH)
        return carry

    lax.fori_loop(1, dp, greet_dp, 0)
    for k in range(1, feat):
        pl.semaphore_signal(
            barrier, inc=1, device_id=at(i, (f + k) % feat), device_id_type=MESH
        )

    slot_row = rslot[...]
    loads[0].wait()
    feats_here = feats[...]

    def pick_plane(plane, carry):
        base = plane * plane_slots
        pick = as_bf16(slot_row - base == iota((plane_slots, rows), 0))
        picked = dot_nn(pick, feats_here).astype(BF16)
        send_x[pl.ds(plane * plane_owners, plane_owners)] = picked.reshape(
            plane_owners, cap, feats.shape[1]
        )
        return carry

    lax.fori_loop(0, planes, pick_plane, 0)
    pl.semaphore_wait(barrier, dp - 1 + feat - 1)

    def send_feats(owner):
        pltpu.make_async_remote_copy(
            src_ref=send_x.at[owner],
            dst_ref=recv_x.at[i],
            send_sem=sx,
            recv_sem=rx,
            device_id=at(owner),
            device_id_type=MESH,
        ).start()

    def send_far(q, carry):
        for k in sorted(range(1, planes), key=lambda k: -min(k, planes - k)):
            send_feats(((z + k) % planes) * plane_owners + (i + q) % plane_owners)
        return carry

    def send_near(q, carry):
        send_feats(z * plane_owners + (i + q) % plane_owners)
        return carry

    lax.fori_loop(0, plane_owners, send_far, 0)
    lax.fori_loop(1, plane_owners, send_near, 0)
    recv_x[i] = send_x[i]

    group_rows = feat * rows
    step = min(512, rows)
    loads[1].wait()
    coef_top, coef_low = split2(fc[...])
    coef_parts[:block_count] = coef_top
    coef_parts[block_count:] = coef_low
    loads[2].wait()

    def partial_chunk(q, carry):
        start = pl.multiple_of(q * step, step)
        values = fv[pl.ds(start, step), :]
        scores = dot_nt(coef_parts[...], values)
        scores = scores[:block_count] + scores[block_count:]
        hot = as_f32(fb[:, pl.ds(start, step)] == iota((block_count, step), 0))
        hot_all[:, pl.ds(start, step)] = hot.astype(BF16)
        part = jnp.sum(scores * hot, axis=0, keepdims=True)
        per = rows // step
        inner = pl.multiple_of((q % per) * step, step)
        send_p[q // per, :, pl.ds(inner, step)] = part
        return carry

    lax.fori_loop(0, group_rows // step, partial_chunk, 0)
    for k in range(1, feat):
        other = (f + k) % feat
        pltpu.make_async_remote_copy(
            src_ref=send_p.at[other],
            dst_ref=recv_p.at[f],
            send_sem=sp,
            recv_sem=rp,
            device_id=at(i, other),
            device_id_type=MESH,
        ).start()
    recv_p[f] = send_p[f]

    positions = tsrc.shape[0]
    tile = iota((1, positions), 1) >> (TILE.bit_length() - 1)
    members = mcoef.shape[0]
    member = jnp.zeros((1, positions), jnp.int32)
    end = jnp.int32(0)
    for m in range(members):
        end = end + mtiles[m]
        member = member + jnp.where(tile >= end, 1, 0)
    source = tsrc[...].reshape(1, positions)
    code = (member << cap_bits) + (source & (cap - 1))
    code_hot = as_bf16(code == iota((members * cap, positions), 0))
    sender_hot = as_bf16((source >> cap_bits) == iota((dp, positions), 0))
    counted = dot_nt(code_hot, sender_hot).astype(BF16)
    spread = as_bf16((iota((dp, slots), 1) >> cap_bits) == iota((dp, slots), 0))
    slot_mask = as_f32((iota((cap, slots), 1) & (cap - 1)) == iota((cap, slots), 0))
    widened = dot_nn(counted, spread)
    for m in range(members):
        member_mask[pl.ds(m, 1), :] = jnp.sum(
            widened[m * cap : (m + 1) * cap] * slot_mask, axis=0, keepdims=True
        )

    owner_hot = as_bf16((slot_row >> cap_bits) == iota((dp, rows), 0))
    slot_hot = as_f32((slot_row & (cap - 1)) == iota((cap, rows), 0))
    label_row = labels[...].astype(F32)
    zeros_row = jnp.zeros((LANES - 2 * cap, rows), BF16)

    wait_all(recv_p.at[pl.ds(0, feat - 1)], rp)
    fixed_score = recv_p[0]
    for k in range(1, feat):
        fixed_score = fixed_score + recv_p[k]

    sent = fixed_score.astype(BF16).astype(F32)
    payload = jnp.concatenate(
        [(slot_hot * sent).astype(BF16), (slot_hot * label_row).astype(BF16), zeros_row], axis=0
    )
    scattered = dot_nt(owner_hot, payload)
    send_s[...] = scattered.reshape(dp, 1, LANES)

    def send_score(k, carry):
        owner = (i + k) % dp
        pltpu.make_async_remote_copy(
            src_ref=send_s.at[owner],
            dst_ref=recv_s.at[i],
            send_sem=ss,
            recv_sem=rs,
            device_id=at(owner),
            device_id_type=MESH,
        ).start()
        return carry

    lax.fori_loop(1, dp, send_score, 0)
    recv_s[i] = send_s[i]
    wait_all(recv_x.at[pl.ds(0, dp - 1)], rx)
    wait_all(recv_s.at[pl.ds(0, dp - 1)], rs)

    mask = member_mask[...]
    got = recv_x[...].reshape(slots, feats.shape[1])
    arrived = recv_s[...].reshape(dp, LANES)[:, : 2 * cap].astype(BF16)
    expanded = dot_tn(arrived, spread)
    score_row = jnp.sum(expanded[:cap] * slot_mask, axis=0, keepdims=True)
    answer_row = jnp.sum(expanded[cap:] * slot_mask, axis=0, keepdims=True)

    def project(vectors):
        top, low = split2(vectors)
        dots = dot_nt(jnp.concatenate([top, low], axis=0), got)
        return jnp.sum((dots[:members] + dots[members:]) * mask, axis=0, keepdims=True)

    def gather_rows(weights):
        top, low = split2(mask * weights)
        sums = dot_nn(jnp.concatenate([top, low], axis=0), got)
        return sums[:members] + sums[members:]

    coef = mcoef[...]
    probability = 1.0 / (1.0 + jnp.exp(-(score_row + project(coef))))
    weight = probability * (1.0 - probability)
    gradient = gather_rows(answer_row - probability) - RIDGE_MEMBER * coef
    got_wide = got.astype(F32)
    square_top, square_low = split2(got_wide * got_wide)
    weight_top, weight_low = split2(mask * weight)
    first = dot_nn(jnp.concatenate([weight_top, weight_low], axis=0), square_top)
    second = dot_nn(weight_top, square_low)
    diagonal = first[:members] + first[members:] + second + RIDGE_MEMBER
    step_sum = jnp.zeros_like(coef)
    remain = gradient
    scaled = remain / diagonal
    search = scaled
    inner_product = jnp.sum(remain * scaled, axis=1, keepdims=True)
    for iteration in range(CG_ITERS):
        image = gather_rows(weight * project(search)) + RIDGE_MEMBER * search
        alpha = inner_product / jnp.sum(search * image, axis=1, keepdims=True)
        step_sum = step_sum + alpha * search
        if iteration + 1 < CG_ITERS:
            remain = remain - alpha * image
            scaled = remain / diagonal
            inner_next = jnp.sum(remain * scaled, axis=1, keepdims=True)
            search = scaled + (inner_next / inner_product) * search
            inner_product = inner_next
    updated = coef + step_sum
    coef_out[...] = updated

    new_top, new_low = split2(project(updated))
    stacked = jnp.concatenate([spread * new_top, spread * new_low], axis=0)
    slot_wide = as_bf16((iota((LANES, slots), 1) & (cap - 1)) == iota((LANES, slots), 0))
    folded = dot_nt(stacked, slot_wide)
    send_r[...] = (folded[:dp] + folded[dp:]).reshape(dp, 1, LANES)

    def send_back(k, carry):
        sender = (i + k) % dp
        pltpu.make_async_remote_copy(
            src_ref=send_r.at[sender],
            dst_ref=recv_r.at[i],
            send_sem=sr,
            recv_sem=rr,
            device_id=at(sender),
            device_id_type=MESH,
        ).start()
        return carry

    lax.fori_loop(1, dp, send_back, 0)
    recv_r[i] = send_r[i]
    wait_all(recv_r.at[pl.ds(0, dp - 1)], rr)
    back_top, back_low = split2(recv_r[...].reshape(dp, LANES)[:, :cap])
    looked = dot_tn(back_top, owner_hot) + dot_tn(back_low, owner_hot)
    member_score = jnp.sum(looked * slot_hot, axis=0, keepdims=True)
    margin = fixed_score + member_score
    margin_out[...] = margin
    send_e[...] = label_row - 1.0 / (1.0 + jnp.exp(-margin))
    for k in range(1, feat):
        other = (f + k) % feat
        pltpu.make_async_remote_copy(
            src_ref=send_e,
            dst_ref=recv_e.at[f],
            send_sem=se.at[k - 1],
            recv_sem=re,
            device_id=at(i, other),
            device_id_type=MESH,
        ).start()
    recv_e[f] = send_e[...]
    wait_all(recv_e.at[pl.ds(0, feat - 1)], re)

    half = block_count // cores

    def gradient_rows(start):
        def add_chunk(q, total):
            first_row = pl.multiple_of(q * rows, rows)
            top, low = split2(recv_e[q])
            hot = hot_all[pl.ds(start, half), pl.ds(first_row, rows)]
            weighted = jnp.concatenate([hot * top, hot * low], axis=0)
            sums = dot_nn(weighted, fv[pl.ds(first_row, rows), :])
            return total + (sums[:half] + sums[half:])

        acc[pl.ds(start, half), :] = lax.fori_loop(
            0, feat, add_chunk, jnp.zeros((half, block_width), F32)
        )

    partner = z * plane_owners + x * cores + (1 - c)
    theirs = pl.multiple_of((1 - c) * half, half)
    mine = pl.multiple_of(c * half, half)
    gradient_rows(theirs)
    core_copy = pltpu.make_async_remote_copy(
        src_ref=acc.at[pl.ds(theirs, half)],
        dst_ref=recv_c,
        send_sem=sc,
        recv_sem=rc,
        device_id=at(partner),
        device_id_type=MESH,
    )
    core_copy.start()
    gradient_rows(mine)
    core_copy.wait_recv()
    acc[pl.ds(mine, half), :] = acc[pl.ds(mine, half), :] + recv_c[...]

    lane = planes * chips
    me = z * chips + x
    share_rows, share_width = half * 2 // lane, block_width // 2

    def device_of(p):
        return at((p // chips) * plane_owners + (p % chips) * cores + c)

    def encode(values, codes, scales, p):
        most = jnp.max(jnp.max(jnp.abs(values), axis=1, keepdims=True), axis=0, keepdims=True)
        most = jnp.maximum(most, 1e-30)
        codes[p] = jnp.round(values * (32767.0 / most)).astype(jnp.int32).astype(jnp.int16)
        scales[p] = jnp.broadcast_to(most * (1.0 / 32767.0), (1, LANES))

    def decode(codes, scales, p):
        return codes[p].astype(jnp.int32).astype(F32) * scales[p][:, :1]

    for p in range(lane):
        rows_of = pl.ds(pl.multiple_of(mine + (p // 2) * share_rows, share_rows), share_rows)
        values = acc[rows_of, (p % 2) * share_width : (p % 2 + 1) * share_width]
        encode(values, send_q, send_k, p)

    def send_share(k, carry):
        p = (me + k) % lane
        for source, target, sems in ((send_q, recv_q, 0), (send_k, recv_k, 1)):
            pltpu.make_async_remote_copy(
                src_ref=source.at[p],
                dst_ref=target.at[me],
                send_sem=sq.at[sems],
                recv_sem=rq.at[sems],
                device_id=device_of(p),
                device_id_type=MESH,
            ).start()
        return carry

    lax.fori_loop(1, lane, send_share, 0)
    recv_q[me] = send_q[me]
    recv_k[me] = send_k[me]
    wait_all(recv_q.at[pl.ds(0, lane - 1)], rq.at[0])
    wait_all(recv_k.at[pl.ds(0, lane - 1)], rq.at[1])
    total = decode(recv_q, recv_k, 0)
    for p in range(1, lane):
        total = total + decode(recv_q, recv_k, p)
    my_rows = pl.ds(pl.multiple_of(mine + (me // 2) * share_rows, share_rows), share_rows)
    my_columns = pl.ds(pl.multiple_of((me % 2) * share_width, share_width), share_width)
    finished = RIDGE_FIXED * fc[my_rows, my_columns] - total / dp
    encode(finished, full_q.at[c], full_k.at[c], me)

    def send_finished(k, carry):
        p = (me + k) % lane
        for source, sems in ((full_q, 0), (full_k, 1)):
            pltpu.make_async_remote_copy(
                src_ref=source.at[c, me],
                dst_ref=source.at[c, me],
                send_sem=sg.at[sems],
                recv_sem=rg.at[sems],
                device_id=device_of(p),
                device_id_type=MESH,
            ).start()
        return carry

    lax.fori_loop(1, lane, send_finished, 0)
    wait_all(full_q.at[c, pl.ds(0, lane - 1)], rg.at[0])
    wait_all(full_k.at[c, pl.ds(0, lane - 1)], rg.at[1])
    last = [
        pltpu.make_async_remote_copy(
            src_ref=source.at[c],
            dst_ref=source.at[c],
            send_sem=sgc.at[sems],
            recv_sem=rgc.at[sems],
            device_id=at(partner),
            device_id_type=MESH,
        )
        for source, sems in ((full_q, 0), (full_k, 1))
    ]
    for copy in last:
        copy.start()

    def write_half(core):
        for p in range(lane):
            first_row = core * half + (p // 2) * share_rows
            grad_out[
                pl.ds(pl.multiple_of(first_row, share_rows), share_rows),
                (p % 2) * share_width : (p % 2 + 1) * share_width,
            ] = decode(full_q.at[core], full_k.at[core], p)

    write_half(c)
    for copy in last:
        copy.wait()
    write_half(1 - c)

    wait_all(send_x.at[pl.ds(0, dp - 1)], sx)
    wait_all(send_p.at[pl.ds(0, feat - 1)], sp)
    wait_all(send_s.at[pl.ds(0, dp - 1)], ss)
    wait_all(send_r.at[pl.ds(0, dp - 1)], sr)
    for k in range(1, feat):
        wait_all(send_e, se.at[k - 1])
    core_copy.wait_send()
    wait_all(send_q.at[pl.ds(0, lane - 1)], sq.at[0])
    wait_all(send_k.at[pl.ds(0, lane - 1)], sq.at[1])
    wait_all(full_q.at[c, pl.ds(0, lane - 1)], sg.at[0])
    wait_all(full_k.at[c, pl.ds(0, lane - 1)], sg.at[1])


def hand_over(margin, updated, grad, margin_out, updated_out, grad_out):
    margin_out[...] = margin[...]
    updated_out[...] = updated[...]
    grad_out[...] = grad[...]


def body(
    member_feats,
    labels,
    fixed_values,
    fixed_blocks,
    fixed_coef,
    member_coef,
    row_slot,
    tile_source,
    member_tiles,
):
    dp = lax.axis_size("dp")
    feat = lax.axis_size("feat")
    planes, chips, cores = grid_of(dp)
    rows, width = member_feats.shape
    members = member_coef.shape[0]
    block_count, block_width = fixed_coef.shape
    cap = 2 * rows // dp
    half = block_count // cores
    lane = planes * chips
    share = (half * 2 // lane, block_width // 2)
    vmem = pl.BlockSpec(memory_space=pltpu.VMEM)
    hbm = pl.BlockSpec(memory_space=pl.ANY)
    smem = pl.BlockSpec(memory_space=pltpu.SMEM)
    dma = pltpu.SemaphoreType.DMA
    margin, updated, grad = pl.pallas_call(
        functools.partial(kernel, dp, feat, cap),
        out_shape=(
            jax.ShapeDtypeStruct((1, rows), F32),
            jax.ShapeDtypeStruct((members, width), F32),
            jax.ShapeDtypeStruct((block_count, block_width), F32),
        ),
        in_specs=[hbm, vmem, hbm, vmem, hbm, vmem, vmem, vmem, smem],
        out_specs=(vmem, vmem, vmem),
        scratch_shapes=[
            pltpu.VMEM((rows, width), BF16),
            pltpu.VMEM(fixed_values.shape, BF16),
            pltpu.VMEM((block_count, block_width), F32),
            pltpu.VMEM((block_count, feat * rows), BF16),
            pltpu.VMEM((dp, cap, width), BF16),
            pltpu.VMEM((dp, cap, width), BF16),
            pltpu.VMEM((feat, 1, rows), F32),
            pltpu.VMEM((feat, 1, rows), F32),
            pltpu.VMEM((dp, 1, LANES), F32),
            pltpu.VMEM((dp, 1, LANES), F32),
            pltpu.VMEM((dp, 1, LANES), F32),
            pltpu.VMEM((dp, 1, LANES), F32),
            pltpu.VMEM((1, rows), F32),
            pltpu.VMEM((feat, 1, rows), F32),
            pltpu.VMEM((2 * block_count, block_width), BF16),
            pltpu.VMEM((members, dp * cap), F32),
            pltpu.VMEM((block_count, block_width), F32),
            pltpu.VMEM((half, block_width), F32),
            pltpu.VMEM((lane, *share), jnp.int16),
            pltpu.VMEM((lane, *share), jnp.int16),
            pltpu.VMEM((cores, lane, *share), jnp.int16),
            pltpu.VMEM((lane, 1, LANES), F32),
            pltpu.VMEM((lane, 1, LANES), F32),
            pltpu.VMEM((cores, lane, 1, LANES), F32),
            dma,
            dma,
            dma,
            dma,
            dma,
            dma,
            dma,
            dma,
            dma((feat - 1,)),
            dma,
            dma,
            dma,
            dma((2,)),
            dma((2,)),
            dma((2,)),
            dma((2,)),
            dma((2,)),
            dma((2,)),
            dma((3,)),
        ],
        compiler_params=pltpu.CompilerParams(
            collective_id=0, has_side_effects=True, vmem_limit_bytes=56 * 2**20
        ),
    )(
        member_feats,
        labels.reshape(1, rows),
        fixed_values,
        fixed_blocks.reshape(1, feat * rows),
        fixed_coef,
        member_coef,
        row_slot.reshape(1, rows),
        tile_source,
        member_tiles,
    )
    margin, updated, grad = pl.pallas_call(
        hand_over,
        out_shape=(
            jax.ShapeDtypeStruct((1, rows), F32),
            jax.ShapeDtypeStruct((members, width), F32),
            jax.ShapeDtypeStruct((block_count, block_width), F32),
        ),
        in_specs=[vmem] * 3,
        out_specs=(vmem,) * 3,
    )(margin, updated, grad)
    return margin.reshape(rows), updated, grad


def solution(mesh):
    placed = (
        P(("dp", "feat"), None),
        P(("dp", "feat")),
        P("dp", "feat"),
        P("dp", "feat"),
        P("feat", None),
        P(("dp", "feat"), None),
        P(("dp", "feat")),
        P(("dp", "feat")),
        P(("dp", "feat")),
    )
    return jax.shard_map(
        body,
        mesh=mesh,
        in_specs=placed,
        out_specs=(P(("dp", "feat")), P(("dp", "feat"), None), P("feat", None)),
        check_vma=False,
    )
```

```python
import functools

import jax
import jax.numpy as jnp
from jax import lax
from jax.experimental import pallas as pl
from jax.experimental.pallas import tpu as pltpu
from jax.sharding import PartitionSpec as P

CG_ITERS = 2
TILE = 128
LANES = 128
RIDGE_MEMBER = 1.0
RIDGE_FIXED = 1.0
F32 = jnp.float32
BF16 = jnp.bfloat16
MESH = pl.DeviceIdType.MESH


def dot_nn(a, b):
    return lax.dot_general(a, b, (((1,), (0,)), ((), ())), preferred_element_type=F32)


def dot_nt(a, b):
    return lax.dot_general(a, b, (((1,), (1,)), ((), ())), preferred_element_type=F32)


def dot_tn(a, b):
    return lax.dot_general(a, b, (((0,), (0,)), ((), ())), preferred_element_type=F32)


def split2(x):
    top = x.astype(BF16)
    return top, (x - top.astype(F32)).astype(BF16)


def iota(shape, dim):
    return lax.broadcasted_iota(jnp.int32, shape, dim)


def as_bf16(mask):
    return jnp.where(mask, 1.0, 0.0).astype(BF16)


def as_f32(mask):
    return jnp.where(mask, 1.0, 0.0).astype(F32)


def decode(codes, scale):
    values = codes.astype(jnp.int32).astype(F32)
    return values * jnp.concatenate([scale] * (values.shape[1] // LANES), axis=1)


def grid_of(dp):
    return (8, 4, 2) if dp == 64 else (dp // 4, 2, 2)


def kernel(
    dp,
    feat,
    cap,
    feats_hbm,
    labels,
    fv_hbm,
    fb,
    fc_hbm,
    mcoef,
    rslot,
    tsrc,
    mtiles,
    margin_out,
    coef_out,
    full_q,
    full_k,
    feats,
    fv,
    fc,
    hot_all,
    send_x,
    recv_x,
    send_p,
    recv_p,
    send_s,
    recv_s,
    send_r,
    recv_r,
    send_e,
    recv_e,
    coef_parts,
    member_mask,
    acc,
    recv_c,
    send_q,
    recv_q,
    send_k,
    recv_k,
    sx,
    rx,
    sp,
    rp,
    ss,
    rs,
    sr,
    rr,
    se,
    re,
    sc,
    rc,
    sq,
    rq,
    sg,
    rg,
    sgc,
    rgc,
    s_load,
):
    planes, chips, cores = grid_of(dp)
    rows = feats.shape[0]
    slots = dp * cap
    cap_bits = cap.bit_length() - 1
    block_count, block_width = fc.shape
    plane_owners = chips * cores
    plane_slots = plane_owners * cap
    i = lax.axis_index("dp")
    f = lax.axis_index("feat")
    z = i // plane_owners
    x = (i % plane_owners) // cores
    c = i % cores

    def at(dp_index, feat_index=None):
        return (dp_index, f if feat_index is None else feat_index)

    def wait_all(ref, sem):
        pltpu.make_async_copy(ref, ref, sem).wait()

    loads = [
        pltpu.make_async_copy(source, target, s_load.at[k])
        for k, (source, target) in enumerate(((feats_hbm, feats), (fc_hbm, fc), (fv_hbm, fv)))
    ]
    for load in loads:
        load.start()

    barrier = pltpu.get_barrier_semaphore()

    def greet_dp(k, carry):
        pl.semaphore_signal(barrier, inc=1, device_id=at((i + k) % dp), device_id_type=MESH)
        return carry

    lax.fori_loop(1, dp, greet_dp, 0)
    for k in range(1, feat):
        pl.semaphore_signal(
            barrier, inc=1, device_id=at(i, (f + k) % feat), device_id_type=MESH
        )

    slot_row = rslot[...]
    loads[0].wait()
    feats_here = feats[...]

    def pick_plane(plane, carry):
        base = plane * plane_slots
        pick = as_bf16(slot_row - base == iota((plane_slots, rows), 0))
        picked = dot_nn(pick, feats_here).astype(BF16)
        send_x[pl.ds(plane * plane_owners, plane_owners)] = picked.reshape(
            plane_owners, cap, feats.shape[1]
        )
        return carry

    lax.fori_loop(0, planes, pick_plane, 0)
    pl.semaphore_wait(barrier, dp - 1 + feat - 1)

    def send_feats(owner):
        pltpu.make_async_remote_copy(
            src_ref=send_x.at[owner],
            dst_ref=recv_x.at[i],
            send_sem=sx,
            recv_sem=rx,
            device_id=at(owner),
            device_id_type=MESH,
        ).start()

    def send_far(q, carry):
        for k in sorted(range(1, planes), key=lambda k: -min(k, planes - k)):
            send_feats(((z + k) % planes) * plane_owners + (i + q) % plane_owners)
        return carry

    def send_near(q, carry):
        send_feats(z * plane_owners + (i + q) % plane_owners)
        return carry

    lax.fori_loop(0, plane_owners, send_far, 0)
    lax.fori_loop(1, plane_owners, send_near, 0)
    recv_x[i] = send_x[i]

    group_rows = feat * rows
    step = min(512, rows)
    loads[1].wait()
    coef_top, coef_low = split2(fc[...])
    coef_parts[:block_count] = coef_top
    coef_parts[block_count:] = coef_low
    loads[2].wait()

    def partial_chunk(q, carry):
        start = pl.multiple_of(q * step, step)
        values = fv[pl.ds(start, step), :]
        scores = dot_nt(coef_parts[...], values)
        scores = scores[:block_count] + scores[block_count:]
        hot = as_f32(fb[:, pl.ds(start, step)] == iota((block_count, step), 0))
        hot_all[:, pl.ds(start, step)] = hot.astype(BF16)
        part = jnp.sum(scores * hot, axis=0, keepdims=True)
        per = rows // step
        inner = pl.multiple_of((q % per) * step, step)
        send_p[q // per, :, pl.ds(inner, step)] = part
        return carry

    lax.fori_loop(0, group_rows // step, partial_chunk, 0)
    for k in range(1, feat):
        other = (f + k) % feat
        pltpu.make_async_remote_copy(
            src_ref=send_p.at[other],
            dst_ref=recv_p.at[f],
            send_sem=sp,
            recv_sem=rp,
            device_id=at(i, other),
            device_id_type=MESH,
        ).start()
    recv_p[f] = send_p[f]

    positions = tsrc.shape[0]
    tile = iota((1, positions), 1) >> (TILE.bit_length() - 1)
    members = mcoef.shape[0]
    member = jnp.zeros((1, positions), jnp.int32)
    end = jnp.int32(0)
    for m in range(members):
        end = end + mtiles[m]
        member = member + jnp.where(tile >= end, 1, 0)
    source = tsrc[...].reshape(1, positions)
    code = (member << cap_bits) + (source & (cap - 1))
    code_hot = as_bf16(code == iota((members * cap, positions), 0))
    sender_hot = as_bf16((source >> cap_bits) == iota((dp, positions), 0))
    counted = dot_nt(code_hot, sender_hot).astype(BF16)
    spread = as_bf16((iota((dp, slots), 1) >> cap_bits) == iota((dp, slots), 0))
    slot_mask = as_f32((iota((cap, slots), 1) & (cap - 1)) == iota((cap, slots), 0))
    widened = dot_nn(counted, spread)
    for m in range(members):
        member_mask[pl.ds(m, 1), :] = jnp.sum(
            widened[m * cap : (m + 1) * cap] * slot_mask, axis=0, keepdims=True
        )

    share_of = LANES // cap
    owner_hot = as_bf16((slot_row >> cap_bits) == iota((dp, rows), 0))
    slot_hot = as_f32((slot_row & (cap - 1)) == iota((cap, rows), 0))
    label_row = labels[...].astype(F32)
    zeros_row = jnp.zeros((LANES - 2 * cap, rows), BF16)

    wait_all(recv_p.at[pl.ds(0, feat - 1)], rp)
    fixed_score = recv_p[0]
    for k in range(1, feat):
        fixed_score = fixed_score + recv_p[k]

    sent = fixed_score.astype(BF16).astype(F32)
    payload = jnp.concatenate(
        [(slot_hot * sent).astype(BF16), (slot_hot * label_row).astype(BF16), zeros_row], axis=0
    )
    scattered = dot_nt(owner_hot, payload)
    send_s[...] = scattered.reshape(dp, 1, LANES)

    def send_score(k, carry):
        owner = (i + k) % dp
        pltpu.make_async_remote_copy(
            src_ref=send_s.at[owner],
            dst_ref=recv_s.at[i],
            send_sem=ss,
            recv_sem=rs,
            device_id=at(owner),
            device_id_type=MESH,
        ).start()
        return carry

    lax.fori_loop(1, dp, send_score, 0)
    recv_s[i] = send_s[i]
    wait_all(recv_s.at[pl.ds(0, dp - 1)], rs)
    arrived = recv_s[...].reshape(dp, LANES)[:, : 2 * cap].astype(BF16)
    expanded = dot_tn(arrived, spread)
    score_row = jnp.sum(expanded[:cap] * slot_mask, axis=0, keepdims=True)
    answer_row = jnp.sum(expanded[cap:] * slot_mask, axis=0, keepdims=True)
    mask = member_mask[...]
    lane_hot = as_f32((slot_row & (cap - 1)) + (i % share_of) * cap == iota((LANES, rows), 0))
    wait_all(recv_x.at[pl.ds(0, dp - 1)], rx)

    got = recv_x[...].reshape(slots, feats.shape[1])

    def project(vectors):
        top, low = split2(vectors)
        dots = dot_nt(jnp.concatenate([top, low], axis=0), got)
        return jnp.sum((dots[:members] + dots[members:]) * mask, axis=0, keepdims=True)

    def gather_rows(weights):
        top, low = split2(mask * weights)
        sums = dot_nn(jnp.concatenate([top, low], axis=0), got)
        return sums[:members] + sums[members:]

    coef = mcoef[...]
    probability = 1.0 / (1.0 + jnp.exp(-(score_row + project(coef))))
    weight = probability * (1.0 - probability)
    gradient = gather_rows(answer_row - probability) - RIDGE_MEMBER * coef
    got_wide = got.astype(F32)
    square_top, square_low = split2(got_wide * got_wide)
    weight_top, weight_low = split2(mask * weight)
    first = dot_nn(jnp.concatenate([weight_top, weight_low], axis=0), square_top)
    second = dot_nn(weight_top, square_low)
    diagonal = first[:members] + first[members:] + second + RIDGE_MEMBER
    step_sum = jnp.zeros_like(coef)
    remain = gradient
    scaled = remain / diagonal
    search = scaled
    inner_product = jnp.sum(remain * scaled, axis=1, keepdims=True)
    for iteration in range(CG_ITERS):
        image = gather_rows(weight * project(search)) + RIDGE_MEMBER * search
        alpha = inner_product / jnp.sum(search * image, axis=1, keepdims=True)
        step_sum = step_sum + alpha * search
        if iteration + 1 < CG_ITERS:
            remain = remain - alpha * image
            scaled = remain / diagonal
            inner_next = jnp.sum(remain * scaled, axis=1, keepdims=True)
            search = scaled + (inner_next / inner_product) * search
            inner_product = inner_next
    updated = coef + step_sum
    coef_out[...] = updated

    new_scores = project(updated)
    for k in range(slots // LANES):
        send_r[k] = new_scores[:, k * LANES : (k + 1) * LANES]

    def send_back(k, carry):
        sender = (i + k) % dp
        pltpu.make_async_remote_copy(
            src_ref=send_r.at[sender // share_of],
            dst_ref=recv_r.at[i],
            send_sem=sr,
            recv_sem=rr,
            device_id=at(sender),
            device_id_type=MESH,
        ).start()
        return carry

    lax.fori_loop(1, dp, send_back, 0)
    recv_r[i] = send_r[i // share_of]
    wait_all(recv_r.at[pl.ds(0, dp - 1)], rr)
    back_top, back_low = split2(recv_r[...].reshape(dp, LANES))
    looked = dot_tn(back_top, owner_hot) + dot_tn(back_low, owner_hot)
    member_score = jnp.sum(looked * lane_hot, axis=0, keepdims=True)
    margin = fixed_score + member_score
    margin_out[...] = margin
    send_e[...] = label_row - 1.0 / (1.0 + jnp.exp(-margin))
    for k in range(1, feat):
        other = (f + k) % feat
        pltpu.make_async_remote_copy(
            src_ref=send_e,
            dst_ref=recv_e.at[f],
            send_sem=se.at[k - 1],
            recv_sem=re,
            device_id=at(i, other),
            device_id_type=MESH,
        ).start()
    recv_e[f] = send_e[...]

    half = block_count // cores

    def quarter(q, start, count):
        first_row = pl.multiple_of(q * rows, rows)
        top, low = split2(recv_e[q])
        hot = hot_all[pl.ds(start, count), pl.ds(first_row, rows)]
        weighted = jnp.concatenate([hot * top, hot * low], axis=0)
        sums = dot_nn(weighted, fv[pl.ds(first_row, rows), :])
        return sums[:count] + sums[count:]

    acc[...] = quarter(f, 0, block_count)
    wait_all(recv_e.at[pl.ds(0, feat - 1)], re)

    def gradient_rows(start):
        acc[pl.ds(start, half), :] = lax.fori_loop(
            1,
            feat,
            lambda k, total: total + quarter((f + k) % feat, start, half),
            acc[pl.ds(start, half), :],
        )

    partner = z * plane_owners + x * cores + (1 - c)
    theirs = pl.multiple_of((1 - c) * half, half)
    mine = pl.multiple_of(c * half, half)
    gradient_rows(theirs)
    core_copy = pltpu.make_async_remote_copy(
        src_ref=acc.at[pl.ds(theirs, half)],
        dst_ref=recv_c,
        send_sem=sc,
        recv_sem=rc,
        device_id=at(partner),
        device_id_type=MESH,
    )
    core_copy.start()
    gradient_rows(mine)
    core_copy.wait_recv()
    acc[pl.ds(mine, half), :] = acc[pl.ds(mine, half), :] + recv_c[...]

    lane = planes * chips
    me = z * chips + x
    share_rows, share_width = half * 2 // lane, block_width // 2

    def device_of(p):
        return at((p // chips) * plane_owners + (p % chips) * cores + c)

    def encode(values, codes, scales, p):
        most = jnp.max(jnp.max(jnp.abs(values), axis=1, keepdims=True), axis=0, keepdims=True)
        most = jnp.maximum(most, 1e-30)
        codes[p] = jnp.round(values * (32767.0 / most)).astype(jnp.int32).astype(jnp.int16)
        scales[p] = jnp.broadcast_to(most * (1.0 / 32767.0), (1, LANES))

    for p in range(lane):
        rows_of = pl.ds(pl.multiple_of(mine + (p // 2) * share_rows, share_rows), share_rows)
        values = acc[rows_of, (p % 2) * share_width : (p % 2 + 1) * share_width]
        encode(values, send_q, send_k, p)

    def send_share(k, carry):
        p = (me + k) % lane
        for source, target, sems in ((send_q, recv_q, 0), (send_k, recv_k, 1)):
            pltpu.make_async_remote_copy(
                src_ref=source.at[p],
                dst_ref=target.at[me],
                send_sem=sq.at[sems],
                recv_sem=rq.at[sems],
                device_id=device_of(p),
                device_id_type=MESH,
            ).start()
        return carry

    lax.fori_loop(1, lane, send_share, 0)
    recv_q[me] = send_q[me]
    recv_k[me] = send_k[me]
    wait_all(recv_q.at[pl.ds(0, lane - 1)], rq.at[0])
    wait_all(recv_k.at[pl.ds(0, lane - 1)], rq.at[1])
    total = decode(recv_q[0], recv_k[0])
    for p in range(1, lane):
        total = total + decode(recv_q[p], recv_k[p])
    my_rows = pl.ds(pl.multiple_of(mine + (me // 2) * share_rows, share_rows), share_rows)
    my_columns = pl.ds(pl.multiple_of((me % 2) * share_width, share_width), share_width)
    finished = RIDGE_FIXED * fc[my_rows, my_columns] - total / dp
    wait_all(send_q.at[pl.ds(0, lane - 1)], sq.at[0])
    wait_all(send_k.at[pl.ds(0, lane - 1)], sq.at[1])
    encode(finished, full_q.at[c], full_k.at[c], me)
    for p in range(lane):
        send_q[p] = full_q[c, me]
        send_k[p] = full_k[c, me]

    def send_finished(k, carry):
        p = (me + k) % lane
        for source, target, sems in ((send_q, full_q, 0), (send_k, full_k, 1)):
            pltpu.make_async_remote_copy(
                src_ref=source.at[p],
                dst_ref=target.at[c, me],
                send_sem=sg.at[sems],
                recv_sem=rg.at[sems],
                device_id=device_of(p),
                device_id_type=MESH,
            ).start()
        return carry

    lax.fori_loop(1, lane, send_finished, 0)
    wait_all(full_q.at[c, pl.ds(0, lane - 1)], rg.at[0])
    wait_all(full_k.at[c, pl.ds(0, lane - 1)], rg.at[1])
    last = [
        pltpu.make_async_remote_copy(
            src_ref=source.at[c],
            dst_ref=source.at[c],
            send_sem=sgc.at[sems],
            recv_sem=rgc.at[sems],
            device_id=at(partner),
            device_id_type=MESH,
        )
        for source, sems in ((full_q, 0), (full_k, 1))
    ]
    for copy in last:
        copy.start()

    for copy in last:
        copy.wait()

    wait_all(send_x.at[pl.ds(0, dp - 1)], sx)
    wait_all(send_p.at[pl.ds(0, feat - 1)], sp)
    wait_all(send_s.at[pl.ds(0, dp - 1)], ss)
    wait_all(recv_r.at[pl.ds(0, dp - 1)], sr)
    for k in range(1, feat):
        wait_all(send_e, se.at[k - 1])
    core_copy.wait_send()
    wait_all(send_q.at[pl.ds(0, lane - 1)], sg.at[0])
    wait_all(send_k.at[pl.ds(0, lane - 1)], sg.at[1])


def write_outputs(margin, updated, codes, scales, margin_out, updated_out, grad_out):
    margin_out[...] = margin[...]
    updated_out[...] = updated[...]
    cores, lane, share_rows, share_width = codes.shape
    for core in range(cores):
        for p in range(lane):
            first_row = (core * lane // 2 + p // 2) * share_rows
            grad_out[
                first_row : first_row + share_rows,
                (p % 2) * share_width : (p % 2 + 1) * share_width,
            ] = decode(codes[core, p], scales[core, p])


def body(
    member_feats,
    labels,
    fixed_values,
    fixed_blocks,
    fixed_coef,
    member_coef,
    row_slot,
    tile_source,
    member_tiles,
):
    dp = lax.axis_size("dp")
    feat = lax.axis_size("feat")
    planes, chips, cores = grid_of(dp)
    rows, width = member_feats.shape
    members = member_coef.shape[0]
    block_count, block_width = fixed_coef.shape
    cap = 2 * rows // dp
    half = block_count // cores
    lane = planes * chips
    share = (half * 2 // lane, block_width // 2)
    vmem = pl.BlockSpec(memory_space=pltpu.VMEM)
    hbm = pl.BlockSpec(memory_space=pl.ANY)
    smem = pl.BlockSpec(memory_space=pltpu.SMEM)
    dma = pltpu.SemaphoreType.DMA
    margin, updated, codes, scales = pl.pallas_call(
        functools.partial(kernel, dp, feat, cap),
        out_shape=(
            jax.ShapeDtypeStruct((1, rows), F32),
            jax.ShapeDtypeStruct((members, width), F32),
            jax.ShapeDtypeStruct((cores, lane, *share), jnp.int16),
            jax.ShapeDtypeStruct((cores, lane, 1, LANES), F32),
        ),
        in_specs=[hbm, vmem, hbm, vmem, hbm, vmem, vmem, vmem, smem],
        out_specs=(vmem,) * 4,
        scratch_shapes=[
            pltpu.VMEM((rows, width), BF16),
            pltpu.VMEM(fixed_values.shape, BF16),
            pltpu.VMEM((block_count, block_width), F32),
            pltpu.VMEM((block_count, feat * rows), BF16),
            pltpu.VMEM((dp, cap, width), BF16),
            pltpu.VMEM((dp, cap, width), BF16),
            pltpu.VMEM((feat, 1, rows), F32),
            pltpu.VMEM((feat, 1, rows), F32),
            pltpu.VMEM((dp, 1, LANES), F32),
            pltpu.VMEM((dp, 1, LANES), F32),
            pltpu.VMEM((dp * cap // LANES, 1, LANES), F32),
            pltpu.VMEM((dp, 1, LANES), F32),
            pltpu.VMEM((1, rows), F32),
            pltpu.VMEM((feat, 1, rows), F32),
            pltpu.VMEM((2 * block_count, block_width), BF16),
            pltpu.VMEM((members, dp * cap), F32),
            pltpu.VMEM((block_count, block_width), F32),
            pltpu.VMEM((half, block_width), F32),
            pltpu.VMEM((lane, *share), jnp.int16),
            pltpu.VMEM((lane, *share), jnp.int16),
            pltpu.VMEM((lane, 1, LANES), F32),
            pltpu.VMEM((lane, 1, LANES), F32),
            dma,
            dma,
            dma,
            dma,
            dma,
            dma,
            dma,
            dma,
            dma((feat - 1,)),
            dma,
            dma,
            dma,
            dma((2,)),
            dma((2,)),
            dma((2,)),
            dma((2,)),
            dma((2,)),
            dma((2,)),
            dma((3,)),
        ],
        compiler_params=pltpu.CompilerParams(
            collective_id=0, has_side_effects=True, vmem_limit_bytes=56 * 2**20
        ),
    )(
        member_feats,
        labels.reshape(1, rows),
        fixed_values,
        fixed_blocks.reshape(1, feat * rows),
        fixed_coef,
        member_coef,
        row_slot.reshape(1, rows),
        tile_source,
        member_tiles,
    )
    margin, updated, grad = pl.pallas_call(
        write_outputs,
        out_shape=(
            jax.ShapeDtypeStruct((1, rows), F32),
            jax.ShapeDtypeStruct((members, width), F32),
            jax.ShapeDtypeStruct((block_count, block_width), F32),
        ),
        in_specs=[vmem] * 4,
        out_specs=(vmem,) * 3,
    )(margin, updated, codes, scales)
    return margin.reshape(rows), updated, grad


def solution(mesh):
    placed = (
        P(("dp", "feat"), None),
        P(("dp", "feat")),
        P("dp", "feat"),
        P("dp", "feat"),
        P("feat", None),
        P(("dp", "feat"), None),
        P(("dp", "feat")),
        P(("dp", "feat")),
        P(("dp", "feat")),
    )
    return jax.shard_map(
        body,
        mesh=mesh,
        in_specs=placed,
        out_specs=(P(("dp", "feat")), P(("dp", "feat"), None), P("feat", None)),
        check_vma=False,
    )
```

```python
import functools

import jax
import jax.numpy as jnp
from jax import lax
from jax.experimental import pallas as pl
from jax.experimental.pallas import tpu as pltpu
from jax.sharding import PartitionSpec as P

CG_ITERS = 2
TILE = 128
LANES = 128
STRIDE = 13
RIDGE_MEMBER = 1.0
RIDGE_FIXED = 1.0
F32 = jnp.float32
BF16 = jnp.bfloat16
MESH = pl.DeviceIdType.MESH


def dot_nn(a, b):
    return lax.dot_general(a, b, (((1,), (0,)), ((), ())), preferred_element_type=F32)


def dot_nt(a, b):
    return lax.dot_general(a, b, (((1,), (1,)), ((), ())), preferred_element_type=F32)


def dot_tn(a, b):
    return lax.dot_general(a, b, (((0,), (0,)), ((), ())), preferred_element_type=F32)


def split2(x):
    top = x.astype(BF16)
    return top, (x - top.astype(F32)).astype(BF16)


def iota(shape, dim):
    return lax.broadcasted_iota(jnp.int32, shape, dim)


def as_bf16(mask):
    return jnp.where(mask, 1.0, 0.0).astype(BF16)


def as_f32(mask):
    return jnp.where(mask, 1.0, 0.0).astype(F32)


def decode(codes, scale):
    values = codes.astype(jnp.int32).astype(F32)
    return values * jnp.concatenate([scale] * (values.shape[1] // LANES), axis=1)


def grid_of(dp):
    return (8, 4, 2) if dp == 64 else (dp // 4, 2, 2)


def kernel(
    dp,
    feat,
    cap,
    feats_hbm,
    labels,
    fv_hbm,
    fb,
    fc_hbm,
    mcoef,
    rslot,
    tsrc,
    mtiles,
    margin_out,
    coef_out,
    full_q,
    full_k,
    feats,
    fv,
    fc,
    hot_all,
    send_x,
    recv_x,
    send_p,
    recv_p,
    send_s,
    recv_s,
    send_r,
    recv_r,
    send_e,
    recv_e,
    coef_parts,
    member_mask,
    acc,
    recv_c,
    send_q,
    recv_q,
    send_k,
    recv_k,
    sx,
    rx,
    sp,
    rp,
    ss,
    rs,
    sr,
    rr,
    se,
    re,
    sc,
    rc,
    sq,
    rq,
    sg,
    rg,
    sgc,
    rgc,
    s_load,
):
    planes, chips, cores = grid_of(dp)
    rows = feats.shape[0]
    slots = dp * cap
    cap_bits = cap.bit_length() - 1
    block_count, block_width = fc.shape
    plane_owners = chips * cores
    plane_slots = plane_owners * cap
    i = lax.axis_index("dp")
    f = lax.axis_index("feat")
    z = i // plane_owners
    x = (i % plane_owners) // cores
    c = i % cores

    def at(dp_index, feat_index=None):
        return (dp_index, f if feat_index is None else feat_index)

    def wait_all(ref, sem):
        pltpu.make_async_copy(ref, ref, sem).wait()

    loads = [
        pltpu.make_async_copy(source, target, s_load.at[k])
        for k, (source, target) in enumerate(((feats_hbm, feats), (fc_hbm, fc), (fv_hbm, fv)))
    ]
    for load in loads:
        load.start()

    barrier = pltpu.get_barrier_semaphore()

    def greet_dp(k, carry):
        pl.semaphore_signal(barrier, inc=1, device_id=at((i + k) % dp), device_id_type=MESH)
        return carry

    lax.fori_loop(1, dp, greet_dp, 0)
    for k in range(1, feat):
        pl.semaphore_signal(
            barrier, inc=1, device_id=at(i, (f + k) % feat), device_id_type=MESH
        )

    slot_row = rslot[...]
    loads[0].wait()
    feats_here = feats[...]

    def pick_plane(plane, carry):
        base = plane * plane_slots
        pick = as_bf16(slot_row - base == iota((plane_slots, rows), 0))
        picked = dot_nn(pick, feats_here).astype(BF16)
        send_x[pl.ds(plane * plane_owners, plane_owners)] = picked.reshape(
            plane_owners, cap, feats.shape[1]
        )
        return carry

    lax.fori_loop(0, planes, pick_plane, 0)
    pl.semaphore_wait(barrier, dp - 1 + feat - 1)

    def send_feats(owner):
        pltpu.make_async_remote_copy(
            src_ref=send_x.at[owner],
            dst_ref=recv_x.at[i],
            send_sem=sx,
            recv_sem=rx,
            device_id=at(owner),
            device_id_type=MESH,
        ).start()

    def send_far(q, carry):
        for k in sorted(range(1, planes), key=lambda k: -min(k, planes - k)):
            send_feats(((z + k) % planes) * plane_owners + (i + q) % plane_owners)
        return carry

    def send_near(q, carry):
        send_feats(z * plane_owners + (i + q) % plane_owners)
        return carry

    lax.fori_loop(0, plane_owners, send_far, 0)
    lax.fori_loop(1, plane_owners, send_near, 0)
    recv_x[i] = send_x[i]

    group_rows = feat * rows
    step = min(512, rows)
    loads[1].wait()
    coef_top, coef_low = split2(fc[...])
    coef_parts[:block_count] = coef_top
    coef_parts[block_count:] = coef_low
    loads[2].wait()

    def partial_chunk(q, carry):
        start = pl.multiple_of(q * step, step)
        values = fv[pl.ds(start, step), :]
        scores = dot_nt(coef_parts[...], values)
        scores = scores[:block_count] + scores[block_count:]
        hot = as_f32(fb[:, pl.ds(start, step)] == iota((block_count, step), 0))
        hot_all[:, pl.ds(start, step)] = hot.astype(BF16)
        part = jnp.sum(scores * hot, axis=0, keepdims=True)
        per = rows // step
        inner = pl.multiple_of((q % per) * step, step)
        send_p[q // per, :, pl.ds(inner, step)] = part
        return carry

    lax.fori_loop(0, group_rows // step, partial_chunk, 0)
    for k in range(1, feat):
        other = (f + k) % feat
        pltpu.make_async_remote_copy(
            src_ref=send_p.at[other],
            dst_ref=recv_p.at[f],
            send_sem=sp,
            recv_sem=rp,
            device_id=at(i, other),
            device_id_type=MESH,
        ).start()
    recv_p[f] = send_p[f]

    positions = tsrc.shape[0]
    tile = iota((1, positions), 1) >> (TILE.bit_length() - 1)
    members = mcoef.shape[0]
    member = jnp.zeros((1, positions), jnp.int32)
    end = jnp.int32(0)
    for m in range(members):
        end = end + mtiles[m]
        member = member + jnp.where(tile >= end, 1, 0)
    source = tsrc[...].reshape(1, positions)
    code = (member << cap_bits) + (source & (cap - 1))
    code_hot = as_bf16(code == iota((members * cap, positions), 0))
    sender_hot = as_bf16((source >> cap_bits) == iota((dp, positions), 0))
    counted = dot_nt(code_hot, sender_hot).astype(BF16)
    spread = as_bf16((iota((dp, slots), 1) >> cap_bits) == iota((dp, slots), 0))
    slot_mask = as_f32((iota((cap, slots), 1) & (cap - 1)) == iota((cap, slots), 0))
    widened = dot_nn(counted, spread)
    for m in range(members):
        member_mask[pl.ds(m, 1), :] = jnp.sum(
            widened[m * cap : (m + 1) * cap] * slot_mask, axis=0, keepdims=True
        )

    share_of = LANES // cap
    owner_hot = as_bf16((slot_row >> cap_bits) == iota((dp, rows), 0))
    slot_hot = as_f32((slot_row & (cap - 1)) == iota((cap, rows), 0))
    label_row = labels[...].astype(F32)
    zeros_row = jnp.zeros((LANES - 2 * cap, rows), BF16)

    wait_all(recv_p.at[pl.ds(0, feat - 1)], rp)
    fixed_score = recv_p[0]
    for k in range(1, feat):
        fixed_score = fixed_score + recv_p[k]

    sent = fixed_score.astype(BF16).astype(F32)
    payload = jnp.concatenate(
        [(slot_hot * sent).astype(BF16), (slot_hot * label_row).astype(BF16), zeros_row], axis=0
    )
    scattered = dot_nt(owner_hot, payload)
    send_s[...] = scattered.reshape(dp, 1, LANES)

    def send_score(k, carry):
        owner = (i + k) % dp
        pltpu.make_async_remote_copy(
            src_ref=send_s.at[owner],
            dst_ref=recv_s.at[i],
            send_sem=ss,
            recv_sem=rs,
            device_id=at(owner),
            device_id_type=MESH,
        ).start()
        return carry

    lax.fori_loop(1, dp, send_score, 0)
    recv_s[i] = send_s[i]
    wait_all(recv_s.at[pl.ds(0, dp - 1)], rs)
    arrived = recv_s[...].reshape(dp, LANES)[:, : 2 * cap].astype(BF16)
    expanded = dot_tn(arrived, spread)
    score_row = jnp.sum(expanded[:cap] * slot_mask, axis=0, keepdims=True)
    answer_row = jnp.sum(expanded[cap:] * slot_mask, axis=0, keepdims=True)
    mask = member_mask[...]
    lane_hot = as_f32((slot_row & (cap - 1)) + (i % share_of) * cap == iota((LANES, rows), 0))
    wait_all(recv_x.at[pl.ds(0, dp - 1)], rx)

    got = recv_x[...].reshape(slots, feats.shape[1])

    def project(vectors):
        top, low = split2(vectors)
        dots = dot_nt(jnp.concatenate([top, low], axis=0), got)
        return jnp.sum((dots[:members] + dots[members:]) * mask, axis=0, keepdims=True)

    def gather_rows(weights):
        top, low = split2(mask * weights)
        sums = dot_nn(jnp.concatenate([top, low], axis=0), got)
        return sums[:members] + sums[members:]

    coef = mcoef[...]
    probability = 1.0 / (1.0 + jnp.exp(-(score_row + project(coef))))
    weight = probability * (1.0 - probability)
    gradient = gather_rows(answer_row - probability) - RIDGE_MEMBER * coef
    got_wide = got.astype(F32)
    square_top, square_low = split2(got_wide * got_wide)
    weight_top, weight_low = split2(mask * weight)
    first = dot_nn(jnp.concatenate([weight_top, weight_low], axis=0), square_top)
    second = dot_nn(weight_top, square_low)
    diagonal = first[:members] + first[members:] + second + RIDGE_MEMBER
    step_sum = jnp.zeros_like(coef)
    remain = gradient
    scaled = remain / diagonal
    search = scaled
    inner_product = jnp.sum(remain * scaled, axis=1, keepdims=True)
    for iteration in range(CG_ITERS):
        image = gather_rows(weight * project(search)) + RIDGE_MEMBER * search
        alpha = inner_product / jnp.sum(search * image, axis=1, keepdims=True)
        step_sum = step_sum + alpha * search
        if iteration + 1 < CG_ITERS:
            remain = remain - alpha * image
            scaled = remain / diagonal
            inner_next = jnp.sum(remain * scaled, axis=1, keepdims=True)
            search = scaled + (inner_next / inner_product) * search
            inner_product = inner_next
    updated = coef + step_sum
    coef_out[...] = updated

    new_scores = project(updated)
    for k in range(slots // LANES):
        send_r[k] = new_scores[:, k * LANES : (k + 1) * LANES]

    def send_back(k, carry):
        sender = (i + k) % dp
        pltpu.make_async_remote_copy(
            src_ref=send_r.at[sender // share_of],
            dst_ref=recv_r.at[i],
            send_sem=sr,
            recv_sem=rr,
            device_id=at(sender),
            device_id_type=MESH,
        ).start()
        return carry

    lax.fori_loop(1, dp, send_back, 0)
    recv_r[i] = send_r[i // share_of]
    wait_all(recv_r.at[pl.ds(0, dp - 1)], rr)
    back_top, back_low = split2(recv_r[...].reshape(dp, LANES))
    looked = dot_tn(back_top, owner_hot) + dot_tn(back_low, owner_hot)
    member_score = jnp.sum(looked * lane_hot, axis=0, keepdims=True)
    margin = fixed_score + member_score
    margin_out[...] = margin
    send_e[...] = label_row - 1.0 / (1.0 + jnp.exp(-margin))
    for k in range(1, feat):
        other = (f + k) % feat
        pltpu.make_async_remote_copy(
            src_ref=send_e,
            dst_ref=recv_e.at[f],
            send_sem=se.at[k - 1],
            recv_sem=re,
            device_id=at(i, other),
            device_id_type=MESH,
        ).start()
    recv_e[f] = send_e[...]

    half = block_count // cores

    def quarter(q, start, count):
        first_row = pl.multiple_of(q * rows, rows)
        top, low = split2(recv_e[q])
        hot = hot_all[pl.ds(start, count), pl.ds(first_row, rows)]
        weighted = jnp.concatenate([hot * top, hot * low], axis=0)
        sums = dot_nn(weighted, fv[pl.ds(first_row, rows), :])
        return sums[:count] + sums[count:]

    acc[...] = quarter(f, 0, block_count)
    wait_all(recv_e.at[pl.ds(0, feat - 1)], re)

    def gradient_rows(start):
        acc[pl.ds(start, half), :] = lax.fori_loop(
            1,
            feat,
            lambda k, total: total + quarter((f + k) % feat, start, half),
            acc[pl.ds(start, half), :],
        )

    partner = z * plane_owners + x * cores + (1 - c)
    theirs = pl.multiple_of((1 - c) * half, half)
    mine = pl.multiple_of(c * half, half)
    gradient_rows(theirs)
    core_copy = pltpu.make_async_remote_copy(
        src_ref=acc.at[pl.ds(theirs, half)],
        dst_ref=recv_c,
        send_sem=sc,
        recv_sem=rc,
        device_id=at(partner),
        device_id_type=MESH,
    )
    core_copy.start()
    gradient_rows(mine)
    core_copy.wait_recv()
    acc[pl.ds(mine, half), :] = acc[pl.ds(mine, half), :] + recv_c[...]

    lane = planes * chips
    me = z * chips + x
    share_rows, share_width = half * 2 // lane, block_width // 2

    def device_of(p):
        return at((p // chips) * plane_owners + (p % chips) * cores + c)

    def encode(values, codes, scales, p):
        most = jnp.max(jnp.max(jnp.abs(values), axis=1, keepdims=True), axis=0, keepdims=True)
        most = jnp.maximum(most, 1e-30)
        codes[p] = jnp.round(values * (32767.0 / most)).astype(jnp.int32).astype(jnp.int16)
        scales[p] = jnp.broadcast_to(most * (1.0 / 32767.0), (1, LANES))

    for p in range(lane):
        rows_of = pl.ds(pl.multiple_of(mine + (p // 2) * share_rows, share_rows), share_rows)
        values = acc[rows_of, (p % 2) * share_width : (p % 2 + 1) * share_width]
        encode(values, send_q, send_k, p)

    def send_share(k, carry):
        p = (me + STRIDE * k) % lane
        for source, target, sems in ((send_k, recv_k, 1), (send_q, recv_q, 0)):
            pltpu.make_async_remote_copy(
                src_ref=source.at[p],
                dst_ref=target.at[me],
                send_sem=sq.at[sems],
                recv_sem=rq.at[sems],
                device_id=device_of(p),
                device_id_type=MESH,
            ).start()
        return carry

    lax.fori_loop(1, lane, send_share, 0)
    recv_q[me] = send_q[me]
    recv_k[me] = send_k[me]
    wait_all(recv_q.at[pl.ds(0, lane - 1)], rq.at[0])
    wait_all(recv_k.at[pl.ds(0, lane - 1)], rq.at[1])
    total = decode(recv_q[0], recv_k[0])
    for p in range(1, lane):
        total = total + decode(recv_q[p], recv_k[p])
    my_rows = pl.ds(pl.multiple_of(mine + (me // 2) * share_rows, share_rows), share_rows)
    my_columns = pl.ds(pl.multiple_of((me % 2) * share_width, share_width), share_width)
    finished = RIDGE_FIXED * fc[my_rows, my_columns] - total / dp
    encode(finished, full_q.at[c], full_k.at[c], me)

    def send_finished(k, carry):
        p = (me + STRIDE * k) % lane
        for source, sems in ((full_k, 1), (full_q, 0)):
            pltpu.make_async_remote_copy(
                src_ref=source.at[c, me],
                dst_ref=source.at[c, me],
                send_sem=sg.at[sems],
                recv_sem=rg.at[sems],
                device_id=device_of(p),
                device_id_type=MESH,
            ).start()
        return carry

    lax.fori_loop(1, lane, send_finished, 0)
    wait_all(full_q.at[c, pl.ds(0, lane - 1)], rg.at[0])
    wait_all(full_k.at[c, pl.ds(0, lane - 1)], rg.at[1])
    last = [
        pltpu.make_async_remote_copy(
            src_ref=source.at[c],
            dst_ref=source.at[c],
            send_sem=sgc.at[sems],
            recv_sem=rgc.at[sems],
            device_id=at(partner),
            device_id_type=MESH,
        )
        for source, sems in ((full_q, 0), (full_k, 1))
    ]
    for copy in last:
        copy.start()

    for copy in last:
        copy.wait()

    wait_all(send_x.at[pl.ds(0, dp - 1)], sx)
    wait_all(send_p.at[pl.ds(0, feat - 1)], sp)
    wait_all(send_s.at[pl.ds(0, dp - 1)], ss)
    wait_all(recv_r.at[pl.ds(0, dp - 1)], sr)
    for k in range(1, feat):
        wait_all(send_e, se.at[k - 1])
    core_copy.wait_send()
    wait_all(send_q.at[pl.ds(0, lane - 1)], sq.at[0])
    wait_all(send_k.at[pl.ds(0, lane - 1)], sq.at[1])
    wait_all(send_q.at[pl.ds(0, lane - 1)], sg.at[0])
    wait_all(send_k.at[pl.ds(0, lane - 1)], sg.at[1])


def write_outputs(margin, updated, codes, scales, margin_out, updated_out, grad_out):
    margin_out[...] = margin[...]
    updated_out[...] = updated[...]
    cores, lane, share_rows, share_width = codes.shape
    for core in range(cores):
        for p in range(lane):
            first_row = (core * lane // 2 + p // 2) * share_rows
            grad_out[
                first_row : first_row + share_rows,
                (p % 2) * share_width : (p % 2 + 1) * share_width,
            ] = decode(codes[core, p], scales[core, p])


def body(
    member_feats,
    labels,
    fixed_values,
    fixed_blocks,
    fixed_coef,
    member_coef,
    row_slot,
    tile_source,
    member_tiles,
):
    dp = lax.axis_size("dp")
    feat = lax.axis_size("feat")
    planes, chips, cores = grid_of(dp)
    rows, width = member_feats.shape
    members = member_coef.shape[0]
    block_count, block_width = fixed_coef.shape
    cap = 2 * rows // dp
    half = block_count // cores
    lane = planes * chips
    share = (half * 2 // lane, block_width // 2)
    vmem = pl.BlockSpec(memory_space=pltpu.VMEM)
    hbm = pl.BlockSpec(memory_space=pl.ANY)
    smem = pl.BlockSpec(memory_space=pltpu.SMEM)
    dma = pltpu.SemaphoreType.DMA
    margin, updated, codes, scales = pl.pallas_call(
        functools.partial(kernel, dp, feat, cap),
        out_shape=(
            jax.ShapeDtypeStruct((1, rows), F32),
            jax.ShapeDtypeStruct((members, width), F32),
            jax.ShapeDtypeStruct((cores, lane, *share), jnp.int16),
            jax.ShapeDtypeStruct((cores, lane, 1, LANES), F32),
        ),
        in_specs=[hbm, vmem, hbm, vmem, hbm, vmem, vmem, vmem, smem],
        out_specs=(vmem,) * 4,
        scratch_shapes=[
            pltpu.VMEM((rows, width), BF16),
            pltpu.VMEM(fixed_values.shape, BF16),
            pltpu.VMEM((block_count, block_width), F32),
            pltpu.VMEM((block_count, feat * rows), BF16),
            pltpu.VMEM((dp, cap, width), BF16),
            pltpu.VMEM((dp, cap, width), BF16),
            pltpu.VMEM((feat, 1, rows), F32),
            pltpu.VMEM((feat, 1, rows), F32),
            pltpu.VMEM((dp, 1, LANES), F32),
            pltpu.VMEM((dp, 1, LANES), F32),
            pltpu.VMEM((dp * cap // LANES, 1, LANES), F32),
            pltpu.VMEM((dp, 1, LANES), F32),
            pltpu.VMEM((1, rows), F32),
            pltpu.VMEM((feat, 1, rows), F32),
            pltpu.VMEM((2 * block_count, block_width), BF16),
            pltpu.VMEM((members, dp * cap), F32),
            pltpu.VMEM((block_count, block_width), F32),
            pltpu.VMEM((half, block_width), F32),
            pltpu.VMEM((lane, *share), jnp.int16),
            pltpu.VMEM((lane, *share), jnp.int16),
            pltpu.VMEM((lane, 1, LANES), F32),
            pltpu.VMEM((lane, 1, LANES), F32),
            dma,
            dma,
            dma,
            dma,
            dma,
            dma,
            dma,
            dma,
            dma((feat - 1,)),
            dma,
            dma,
            dma,
            dma((2,)),
            dma((2,)),
            dma((2,)),
            dma((2,)),
            dma((2,)),
            dma((2,)),
            dma((3,)),
        ],
        compiler_params=pltpu.CompilerParams(
            collective_id=0, has_side_effects=True, vmem_limit_bytes=56 * 2**20
        ),
    )(
        member_feats,
        labels.reshape(1, rows),
        fixed_values,
        fixed_blocks.reshape(1, feat * rows),
        fixed_coef,
        member_coef,
        row_slot.reshape(1, rows),
        tile_source,
        member_tiles,
    )
    margin, updated, grad = pl.pallas_call(
        write_outputs,
        out_shape=(
            jax.ShapeDtypeStruct((1, rows), F32),
            jax.ShapeDtypeStruct((members, width), F32),
            jax.ShapeDtypeStruct((block_count, block_width), F32),
        ),
        in_specs=[vmem] * 4,
        out_specs=(vmem,) * 3,
    )(margin, updated, codes, scales)
    return margin.reshape(rows), updated, grad


def solution(mesh):
    placed = (
        P(("dp", "feat"), None),
        P(("dp", "feat")),
        P("dp", "feat"),
        P("dp", "feat"),
        P("feat", None),
        P(("dp", "feat"), None),
        P(("dp", "feat")),
        P(("dp", "feat")),
        P(("dp", "feat")),
    )
    return jax.shard_map(
        body,
        mesh=mesh,
        in_specs=placed,
        out_specs=(P(("dp", "feat")), P(("dp", "feat"), None), P("feat", None)),
        check_vma=False,
    )
```

```python
import functools

import jax
import jax.numpy as jnp
from jax import lax
from jax.experimental import pallas as pl
from jax.experimental.pallas import tpu as pltpu
from jax.sharding import PartitionSpec as P

CG_ITERS = 2
TILE = 128
LANES = 128
STRIDE = 13
RIDGE_MEMBER = 1.0
RIDGE_FIXED = 1.0
F32 = jnp.float32
BF16 = jnp.bfloat16
MESH = pl.DeviceIdType.MESH


def dot_nn(a, b):
    return lax.dot_general(a, b, (((1,), (0,)), ((), ())), preferred_element_type=F32)


def dot_nt(a, b):
    return lax.dot_general(a, b, (((1,), (1,)), ((), ())), preferred_element_type=F32)


def dot_tn(a, b):
    return lax.dot_general(a, b, (((0,), (0,)), ((), ())), preferred_element_type=F32)


def split2(x):
    top = x.astype(BF16)
    return top, (x - top.astype(F32)).astype(BF16)


def iota(shape, dim):
    return lax.broadcasted_iota(jnp.int32, shape, dim)


def as_bf16(mask):
    return jnp.where(mask, 1.0, 0.0).astype(BF16)


def as_f32(mask):
    return jnp.where(mask, 1.0, 0.0).astype(F32)


def decode(codes, scale):
    values = codes.astype(jnp.int32).astype(F32)
    return values * jnp.concatenate([scale] * (values.shape[1] // LANES), axis=1)


def grid_of(dp):
    return (8, 4, 2) if dp == 64 else (dp // 4, 2, 2)


def kernel(
    dp,
    feat,
    cap,
    feats_hbm,
    labels,
    fv_hbm,
    fb,
    fc_hbm,
    mcoef,
    rslot,
    tsrc,
    mtiles,
    margin_out,
    coef_out,
    full_q,
    full_k,
    feats,
    fv,
    fc,
    hot_all,
    send_x,
    recv_x,
    send_p,
    recv_p,
    send_s,
    recv_s,
    send_r,
    recv_r,
    send_e,
    recv_e,
    coef_parts,
    member_mask,
    side,
    acc,
    recv_c,
    send_q,
    recv_q,
    send_k,
    recv_k,
    sx,
    rx,
    sp,
    rp,
    ss,
    rs,
    sr,
    rr,
    se,
    re,
    sc,
    rc,
    sq,
    rq,
    sg,
    rg,
    sgc,
    rgc,
    s_load,
):
    planes, chips, cores = grid_of(dp)
    rows = feats.shape[0]
    slots = dp * cap
    cap_bits = cap.bit_length() - 1
    block_count, block_width = fc.shape
    plane_owners = chips * cores
    plane_slots = plane_owners * cap
    i = lax.axis_index("dp")
    f = lax.axis_index("feat")
    z = i // plane_owners
    x = (i % plane_owners) // cores
    c = i % cores

    def at(dp_index, feat_index=None):
        return (dp_index, f if feat_index is None else feat_index)

    def wait_all(ref, sem):
        pltpu.make_async_copy(ref, ref, sem).wait()

    loads = [
        pltpu.make_async_copy(source, target, s_load.at[k])
        for k, (source, target) in enumerate(((feats_hbm, feats), (fc_hbm, fc), (fv_hbm, fv)))
    ]
    for load in loads:
        load.start()

    barrier = pltpu.get_barrier_semaphore()

    def greet_dp(k, carry):
        pl.semaphore_signal(barrier, inc=1, device_id=at((i + k) % dp), device_id_type=MESH)
        return carry

    lax.fori_loop(1, dp, greet_dp, 0)
    for k in range(1, feat):
        pl.semaphore_signal(
            barrier, inc=1, device_id=at(i, (f + k) % feat), device_id_type=MESH
        )

    slot_row = rslot[...]
    loads[0].wait()
    feats_here = feats[...]

    def pick_plane(plane, carry):
        base = plane * plane_slots
        pick = as_bf16(slot_row - base == iota((plane_slots, rows), 0))
        picked = dot_nn(pick, feats_here).astype(BF16)
        send_x[pl.ds(plane * plane_owners, plane_owners)] = picked.reshape(
            plane_owners, cap, feats.shape[1]
        )
        return carry

    lax.fori_loop(0, planes, pick_plane, 0)
    pl.semaphore_wait(barrier, dp - 1 + feat - 1)

    def send_feats(owner, k):
        pltpu.make_async_remote_copy(
            src_ref=send_x.at[owner],
            dst_ref=recv_x.at[i],
            send_sem=sx,
            recv_sem=rx.at[k],
            device_id=at(owner),
            device_id_type=MESH,
        ).start()

    def send_far(q, carry):
        for k in sorted(range(1, planes), key=lambda k: -min(k, planes - k)):
            send_feats(((z + k) % planes) * plane_owners + (i + q) % plane_owners, k)
        return carry

    def send_near(q, carry):
        send_feats(z * plane_owners + (i + q) % plane_owners, 0)
        return carry

    lax.fori_loop(0, plane_owners, send_far, 0)
    lax.fori_loop(1, plane_owners, send_near, 0)
    recv_x[i] = send_x[i]

    group_rows = feat * rows
    step = min(512, rows)
    loads[1].wait()
    coef_top, coef_low = split2(fc[...])
    coef_parts[:block_count] = coef_top
    coef_parts[block_count:] = coef_low
    loads[2].wait()

    def partial_chunk(q, carry):
        start = pl.multiple_of(q * step, step)
        values = fv[pl.ds(start, step), :]
        scores = dot_nt(coef_parts[...], values)
        scores = scores[:block_count] + scores[block_count:]
        hot = as_f32(fb[:, pl.ds(start, step)] == iota((block_count, step), 0))
        hot_all[:, pl.ds(start, step)] = hot.astype(BF16)
        part = jnp.sum(scores * hot, axis=0, keepdims=True)
        per = rows // step
        inner = pl.multiple_of((q % per) * step, step)
        send_p[q // per, :, pl.ds(inner, step)] = part
        return carry

    lax.fori_loop(0, group_rows // step, partial_chunk, 0)
    for k in range(1, feat):
        other = (f + k) % feat
        pltpu.make_async_remote_copy(
            src_ref=send_p.at[other],
            dst_ref=recv_p.at[f],
            send_sem=sp,
            recv_sem=rp,
            device_id=at(i, other),
            device_id_type=MESH,
        ).start()
    recv_p[f] = send_p[f]

    positions = tsrc.shape[0]
    tile = iota((1, positions), 1) >> (TILE.bit_length() - 1)
    members = mcoef.shape[0]
    member = jnp.zeros((1, positions), jnp.int32)
    end = jnp.int32(0)
    for m in range(members):
        end = end + mtiles[m]
        member = member + jnp.where(tile >= end, 1, 0)
    source = tsrc[...].reshape(1, positions)
    code = (member << cap_bits) + (source & (cap - 1))
    code_hot = as_bf16(code == iota((members * cap, positions), 0))
    sender_hot = as_bf16((source >> cap_bits) == iota((dp, positions), 0))
    counted = dot_nt(code_hot, sender_hot).astype(BF16)
    spread = as_bf16((iota((dp, slots), 1) >> cap_bits) == iota((dp, slots), 0))
    slot_mask = as_f32((iota((cap, slots), 1) & (cap - 1)) == iota((cap, slots), 0))
    widened = dot_nn(counted, spread)
    for m in range(members):
        member_mask[pl.ds(m, 1), :] = jnp.sum(
            widened[m * cap : (m + 1) * cap] * slot_mask, axis=0, keepdims=True
        )

    share_of = LANES // cap
    owner_hot = as_bf16((slot_row >> cap_bits) == iota((dp, rows), 0))
    slot_hot = as_f32((slot_row & (cap - 1)) == iota((cap, rows), 0))
    label_row = labels[...].astype(F32)
    zeros_row = jnp.zeros((LANES - 2 * cap, rows), BF16)

    wait_all(recv_p.at[pl.ds(0, feat - 1)], rp)
    fixed_score = recv_p[0]
    for k in range(1, feat):
        fixed_score = fixed_score + recv_p[k]

    sent = fixed_score.astype(BF16).astype(F32)
    payload = jnp.concatenate(
        [(slot_hot * sent).astype(BF16), (slot_hot * label_row).astype(BF16), zeros_row], axis=0
    )
    scattered = dot_nt(owner_hot, payload)
    send_s[...] = scattered.reshape(dp, 1, LANES)

    def send_score(k, carry):
        owner = (i + k) % dp
        pltpu.make_async_remote_copy(
            src_ref=send_s.at[owner],
            dst_ref=recv_s.at[i],
            send_sem=ss,
            recv_sem=rs,
            device_id=at(owner),
            device_id_type=MESH,
        ).start()
        return carry

    lax.fori_loop(1, dp, send_score, 0)
    recv_s[i] = send_s[i]
    wait_all(recv_s.at[pl.ds(0, dp - 1)], rs)
    arrived = recv_s[...].reshape(dp, LANES)[:, : 2 * cap].astype(BF16)
    expanded = dot_tn(arrived, spread)
    side[0:1, :] = jnp.sum(expanded[:cap] * slot_mask, axis=0, keepdims=True)
    side[1:2, :] = jnp.sum(expanded[cap:] * slot_mask, axis=0, keepdims=True)
    mask = member_mask[...]
    lane_hot = as_f32((slot_row & (cap - 1)) + (i % share_of) * cap == iota((LANES, rows), 0))
    coef = mcoef[...]
    coef_stack = jnp.concatenate(split2(coef), axis=0)
    gradient = -RIDGE_MEMBER * coef
    diagonal = jnp.full(coef.shape, RIDGE_MEMBER, F32)
    for k in sorted(range(planes), key=lambda k: min(k, planes - k)):
        wait_all(recv_x.at[pl.ds(0, plane_owners - (k == 0))], rx.at[k])
        plane = (z - k + planes) % planes
        span = pl.ds(pl.multiple_of(plane * plane_slots, plane_slots), plane_slots)
        block = recv_x[pl.ds(plane * plane_owners, plane_owners)]
        block = block.reshape(plane_slots, feats.shape[1])
        here = member_mask[:, span]
        dots = dot_nt(coef_stack, block)
        logit = side[0:1, span] + jnp.sum(
            (dots[:members] + dots[members:]) * here, axis=0, keepdims=True
        )
        probability = 1.0 / (1.0 + jnp.exp(-logit))
        slope = probability * (1.0 - probability)
        side[2:3, span] = slope
        left = jnp.concatenate(split2(here * (side[1:2, span] - probability)), axis=0)
        sums = dot_nn(left, block)
        gradient = gradient + (sums[:members] + sums[members:])
        wide = block.astype(F32)
        square_top, square_low = split2(wide * wide)
        slope_top, slope_low = split2(here * slope)
        first = dot_nn(jnp.concatenate([slope_top, slope_low], axis=0), square_top)
        second = dot_nn(slope_top, square_low)
        diagonal = diagonal + (first[:members] + first[members:] + second)

    got = recv_x[...].reshape(slots, feats.shape[1])
    weight = side[2:3, :]

    def project(vectors):
        top, low = split2(vectors)
        dots = dot_nt(jnp.concatenate([top, low], axis=0), got)
        return jnp.sum((dots[:members] + dots[members:]) * mask, axis=0, keepdims=True)

    def gather_rows(weights):
        top, low = split2(mask * weights)
        sums = dot_nn(jnp.concatenate([top, low], axis=0), got)
        return sums[:members] + sums[members:]

    step_sum = jnp.zeros_like(coef)
    remain = gradient
    scaled = remain / diagonal
    search = scaled
    inner_product = jnp.sum(remain * scaled, axis=1, keepdims=True)
    for iteration in range(CG_ITERS):
        image = gather_rows(weight * project(search)) + RIDGE_MEMBER * search
        alpha = inner_product / jnp.sum(search * image, axis=1, keepdims=True)
        step_sum = step_sum + alpha * search
        if iteration + 1 < CG_ITERS:
            remain = remain - alpha * image
            scaled = remain / diagonal
            inner_next = jnp.sum(remain * scaled, axis=1, keepdims=True)
            search = scaled + (inner_next / inner_product) * search
            inner_product = inner_next
    updated = coef + step_sum
    coef_out[...] = updated

    new_scores = project(updated)
    for k in range(slots // LANES):
        send_r[k] = new_scores[:, k * LANES : (k + 1) * LANES]

    def send_back(k, carry):
        sender = (i + k) % dp
        pltpu.make_async_remote_copy(
            src_ref=send_r.at[sender // share_of],
            dst_ref=recv_r.at[i],
            send_sem=sr,
            recv_sem=rr,
            device_id=at(sender),
            device_id_type=MESH,
        ).start()
        return carry

    lax.fori_loop(1, dp, send_back, 0)
    recv_r[i] = send_r[i // share_of]
    wait_all(recv_r.at[pl.ds(0, dp - 1)], rr)
    back_top, back_low = split2(recv_r[...].reshape(dp, LANES))
    looked = dot_tn(back_top, owner_hot) + dot_tn(back_low, owner_hot)
    member_score = jnp.sum(looked * lane_hot, axis=0, keepdims=True)
    margin = fixed_score + member_score
    margin_out[...] = margin
    send_e[...] = label_row - 1.0 / (1.0 + jnp.exp(-margin))
    for k in range(1, feat):
        other = (f + k) % feat
        pltpu.make_async_remote_copy(
            src_ref=send_e,
            dst_ref=recv_e.at[f],
            send_sem=se.at[k - 1],
            recv_sem=re,
            device_id=at(i, other),
            device_id_type=MESH,
        ).start()
    recv_e[f] = send_e[...]

    half = block_count // cores

    def quarter(q, start, count):
        first_row = pl.multiple_of(q * rows, rows)
        top, low = split2(recv_e[q])
        hot = hot_all[pl.ds(start, count), pl.ds(first_row, rows)]
        weighted = jnp.concatenate([hot * top, hot * low], axis=0)
        sums = dot_nn(weighted, fv[pl.ds(first_row, rows), :])
        return sums[:count] + sums[count:]

    acc[...] = quarter(f, 0, block_count)
    wait_all(recv_e.at[pl.ds(0, feat - 1)], re)

    def gradient_rows(start):
        total = acc[pl.ds(start, half), :]
        for k in range(1, feat):
            total = total + quarter((f + k) % feat, start, half)
        acc[pl.ds(start, half), :] = total

    partner = z * plane_owners + x * cores + (1 - c)
    theirs = pl.multiple_of((1 - c) * half, half)
    mine = pl.multiple_of(c * half, half)
    gradient_rows(theirs)
    core_copy = pltpu.make_async_remote_copy(
        src_ref=acc.at[pl.ds(theirs, half)],
        dst_ref=recv_c,
        send_sem=sc,
        recv_sem=rc,
        device_id=at(partner),
        device_id_type=MESH,
    )
    core_copy.start()
    gradient_rows(mine)
    core_copy.wait_recv()
    acc[pl.ds(mine, half), :] = acc[pl.ds(mine, half), :] + recv_c[...]

    lane = planes * chips
    me = z * chips + x
    share_rows, share_width = half * 2 // lane, block_width // 2

    def device_of(p):
        return at((p // chips) * plane_owners + (p % chips) * cores + c)

    def encode(values, codes, scales, p):
        most = jnp.max(jnp.max(jnp.abs(values), axis=1, keepdims=True), axis=0, keepdims=True)
        most = jnp.maximum(most, 1e-30)
        codes[p] = jnp.round(values * (32767.0 / most)).astype(jnp.int32).astype(jnp.int16)
        scales[p] = jnp.broadcast_to(most * (1.0 / 32767.0), (1, LANES))

    for p in range(lane):
        rows_of = pl.ds(pl.multiple_of(mine + (p // 2) * share_rows, share_rows), share_rows)
        values = acc[rows_of, (p % 2) * share_width : (p % 2 + 1) * share_width]
        encode(values, send_q, send_k, p)

    def send_share(k, carry):
        p = (me + STRIDE * k) % lane
        for source, target, sems in ((send_k, recv_k, 1), (send_q, recv_q, 0)):
            pltpu.make_async_remote_copy(
                src_ref=source.at[p],
                dst_ref=target.at[me],
                send_sem=sq.at[sems],
                recv_sem=rq.at[sems],
                device_id=device_of(p),
                device_id_type=MESH,
            ).start()
        return carry

    lax.fori_loop(1, lane, send_share, 0)
    recv_q[me] = send_q[me]
    recv_k[me] = send_k[me]
    wait_all(recv_q.at[pl.ds(0, lane - 1)], rq.at[0])
    wait_all(recv_k.at[pl.ds(0, lane - 1)], rq.at[1])
    total = decode(recv_q[0], recv_k[0])
    for p in range(1, lane):
        total = total + decode(recv_q[p], recv_k[p])
    my_rows = pl.ds(pl.multiple_of(mine + (me // 2) * share_rows, share_rows), share_rows)
    my_columns = pl.ds(pl.multiple_of((me % 2) * share_width, share_width), share_width)
    finished = RIDGE_FIXED * fc[my_rows, my_columns] - total / dp
    encode(finished, full_q.at[c], full_k.at[c], me)

    def send_finished(k, carry):
        p = (me + STRIDE * k) % lane
        for source, sems in ((full_k, 1), (full_q, 0)):
            pltpu.make_async_remote_copy(
                src_ref=source.at[c, me],
                dst_ref=source.at[c, me],
                send_sem=sg.at[sems],
                recv_sem=rg.at[sems],
                device_id=device_of(p),
                device_id_type=MESH,
            ).start()
        return carry

    lax.fori_loop(1, lane, send_finished, 0)
    wait_all(full_q.at[c, pl.ds(0, lane - 1)], rg.at[0])
    wait_all(full_k.at[c, pl.ds(0, lane - 1)], rg.at[1])
    last = [
        pltpu.make_async_remote_copy(
            src_ref=source.at[c],
            dst_ref=source.at[c],
            send_sem=sgc.at[sems],
            recv_sem=rgc.at[sems],
            device_id=at(partner),
            device_id_type=MESH,
        )
        for source, sems in ((full_q, 0), (full_k, 1))
    ]
    for copy in last:
        copy.start()

    for copy in last:
        copy.wait()

    wait_all(send_x.at[pl.ds(0, dp - 1)], sx)
    wait_all(send_p.at[pl.ds(0, feat - 1)], sp)
    wait_all(send_s.at[pl.ds(0, dp - 1)], ss)
    wait_all(recv_r.at[pl.ds(0, dp - 1)], sr)
    for k in range(1, feat):
        wait_all(send_e, se.at[k - 1])
    core_copy.wait_send()
    wait_all(send_q.at[pl.ds(0, lane - 1)], sq.at[0])
    wait_all(send_k.at[pl.ds(0, lane - 1)], sq.at[1])
    wait_all(send_q.at[pl.ds(0, lane - 1)], sg.at[0])
    wait_all(send_k.at[pl.ds(0, lane - 1)], sg.at[1])


def write_outputs(margin, updated, codes, scales, margin_out, updated_out, grad_out):
    margin_out[...] = margin[...]
    updated_out[...] = updated[...]
    cores, lane, share_rows, share_width = codes.shape
    for core in range(cores):
        for p in range(lane):
            first_row = (core * lane // 2 + p // 2) * share_rows
            grad_out[
                first_row : first_row + share_rows,
                (p % 2) * share_width : (p % 2 + 1) * share_width,
            ] = decode(codes[core, p], scales[core, p])


def body(
    member_feats,
    labels,
    fixed_values,
    fixed_blocks,
    fixed_coef,
    member_coef,
    row_slot,
    tile_source,
    member_tiles,
):
    dp = lax.axis_size("dp")
    feat = lax.axis_size("feat")
    planes, chips, cores = grid_of(dp)
    rows, width = member_feats.shape
    members = member_coef.shape[0]
    block_count, block_width = fixed_coef.shape
    cap = 2 * rows // dp
    half = block_count // cores
    lane = planes * chips
    share = (half * 2 // lane, block_width // 2)
    vmem = pl.BlockSpec(memory_space=pltpu.VMEM)
    hbm = pl.BlockSpec(memory_space=pl.ANY)
    smem = pl.BlockSpec(memory_space=pltpu.SMEM)
    dma = pltpu.SemaphoreType.DMA
    margin, updated, codes, scales = pl.pallas_call(
        functools.partial(kernel, dp, feat, cap),
        out_shape=(
            jax.ShapeDtypeStruct((1, rows), F32),
            jax.ShapeDtypeStruct((members, width), F32),
            jax.ShapeDtypeStruct((cores, lane, *share), jnp.int16),
            jax.ShapeDtypeStruct((cores, lane, 1, LANES), F32),
        ),
        in_specs=[hbm, vmem, hbm, vmem, hbm, vmem, vmem, vmem, smem],
        out_specs=(vmem,) * 4,
        scratch_shapes=[
            pltpu.VMEM((rows, width), BF16),
            pltpu.VMEM(fixed_values.shape, BF16),
            pltpu.VMEM((block_count, block_width), F32),
            pltpu.VMEM((block_count, feat * rows), BF16),
            pltpu.VMEM((dp, cap, width), BF16),
            pltpu.VMEM((dp, cap, width), BF16),
            pltpu.VMEM((feat, 1, rows), F32),
            pltpu.VMEM((feat, 1, rows), F32),
            pltpu.VMEM((dp, 1, LANES), F32),
            pltpu.VMEM((dp, 1, LANES), F32),
            pltpu.VMEM((dp * cap // LANES, 1, LANES), F32),
            pltpu.VMEM((dp, 1, LANES), F32),
            pltpu.VMEM((1, rows), F32),
            pltpu.VMEM((feat, 1, rows), F32),
            pltpu.VMEM((2 * block_count, block_width), BF16),
            pltpu.VMEM((members, dp * cap), F32),
            pltpu.VMEM((3, dp * cap), F32),
            pltpu.VMEM((block_count, block_width), F32),
            pltpu.VMEM((half, block_width), F32),
            pltpu.VMEM((lane, *share), jnp.int16),
            pltpu.VMEM((lane, *share), jnp.int16),
            pltpu.VMEM((lane, 1, LANES), F32),
            pltpu.VMEM((lane, 1, LANES), F32),
            dma,
            dma((planes,)),
            dma,
            dma,
            dma,
            dma,
            dma,
            dma,
            dma((feat - 1,)),
            dma,
            dma,
            dma,
            dma((2,)),
            dma((2,)),
            dma((2,)),
            dma((2,)),
            dma((2,)),
            dma((2,)),
            dma((3,)),
        ],
        compiler_params=pltpu.CompilerParams(
            collective_id=0, has_side_effects=True, vmem_limit_bytes=56 * 2**20
        ),
    )(
        member_feats,
        labels.reshape(1, rows),
        fixed_values,
        fixed_blocks.reshape(1, feat * rows),
        fixed_coef,
        member_coef,
        row_slot.reshape(1, rows),
        tile_source,
        member_tiles,
    )
    margin, updated, grad = pl.pallas_call(
        write_outputs,
        out_shape=(
            jax.ShapeDtypeStruct((1, rows), F32),
            jax.ShapeDtypeStruct((members, width), F32),
            jax.ShapeDtypeStruct((block_count, block_width), F32),
        ),
        in_specs=[vmem] * 4,
        out_specs=(vmem,) * 3,
    )(margin, updated, codes, scales)
    return margin.reshape(rows), updated, grad


def solution(mesh):
    placed = (
        P(("dp", "feat"), None),
        P(("dp", "feat")),
        P("dp", "feat"),
        P("dp", "feat"),
        P("feat", None),
        P(("dp", "feat"), None),
        P(("dp", "feat")),
        P(("dp", "feat")),
        P(("dp", "feat")),
    )
    return jax.shard_map(
        body,
        mesh=mesh,
        in_specs=placed,
        out_specs=(P(("dp", "feat")), P(("dp", "feat"), None), P("feat", None)),
        check_vma=False,
    )
```
